256 devices in a mesh: dp: 2 (over core), ctx: 32 (over z, y), head: 4 (over x).
Axes of the slice: x: 4, y: 4, z: 8, core: 2. Of those that a mesh axis runs over, the one named last changes fastest.
Arguments:
- query: bfloat16 [16384, 1024], P(('dp', 'ctx'), 'head'), parts along dimension 0, may hold values from -400 to 400
- key: bfloat16 [16384, 1024], P(('dp', 'ctx'), 'head'), parts along dimension 0, may hold values from -400 to 400
- value: bfloat16 [16384, 2048], P(('dp', 'ctx'), 'head'), parts along dimension 0, may hold values from -6 to 6
- out_grad: bfloat16 [16384, 2048], P(('dp', 'ctx'), 'head'), parts along dimension 0, may hold values from -6 to 6
- log_decay: float32 [16, 16384], P('head', ('dp', 'ctx')), parts along dimension 1, may hold values from -2 to 0
- beta: float32 [16, 16384], P('head', ('dp', 'ctx')), parts along dimension 1, may hold values from 0.05 to 0.95
- w_query: bfloat16 [2048, 1024], P(None, 'head'), may hold values from -0.125 to 0.125
- w_key: bfloat16 [2048, 1024], P(None, 'head'), may hold values from -0.125 to 0.125
- w_value: bfloat16 [2048, 2048], P(None, 'head'), may hold values from -0.125 to 0.125
Outputs:
- input_grad: bfloat16 [16384, 2048], P(('dp', 'ctx', 'head')), parts along dimension 0
- decay_grad: float32 [16, 16384], P('head', ('dp', 'ctx')), parts along dimension 1
- beta_grad: float32 [16, 16384], P('head', ('dp', 'ctx')), parts along dimension 1
The draws below stay inside these ranges and needn't reach their ends.
There are 2 independent parts, one for each index of `dp`. The reference program is written for one: setup_inputs(seed, part) draws one part's arguments, and reference() takes and returns one part's arrays. A program takes and returns all parts, laid end to end along the dimension named above; an argument that names none is the same for every part. Nothing has to cross between parts.
All inputs are finite; a program needn't handle non-finite values.
Results may differ from the reference program's by a relative error of at most 0.0049.
Values sent between devices are 32-bit elements; how exact they have to be, the bound alone decides.
A program may use at most 128 MiB of HBM per device.

```python
import math
from functools import partial
import jax
import jax.numpy as jnp
from jax import lax

D = 2048
VALUE_HEADS = 16
NK = 8
HD = 128
STRETCH = 64
TOKEN_COUNT = 8192


def scatter_entries(seed_key, base_draw):
    row_key, col_key = jax.random.split(seed_key)
    row_scale = jnp.exp(jax.random.uniform(row_key, (TOKEN_COUNT, NK, 1), minval=0.0, maxval=math.log(10.0)))
    col_scale = jnp.exp(jax.random.uniform(col_key, (1, NK, HD), minval=0.0, maxval=math.log(10.0)))
    return (base_draw * row_scale * col_scale).reshape(TOKEN_COUNT, NK * HD).astype(jnp.bfloat16)


def draw_query(key, part):
    key = jax.random.fold_in(key, 3)
    base_key, scale_key = jax.random.split(key)
    base_draw = jax.random.truncated_normal(base_key, -4.0, 4.0, (TOKEN_COUNT, NK, HD))
    return scatter_entries(scale_key, base_draw)


def draw_key(key, part):
    key = jax.random.fold_in(key, 7)
    base_key, scale_key = jax.random.split(key)
    base_draw = jax.random.truncated_normal(base_key, -4.0, 4.0, (TOKEN_COUNT, NK, HD))
    return scatter_entries(scale_key, base_draw)


def draw_log_decay(key, part):
    key = jax.random.fold_in(key, 11)
    key_rows = jax.random.split(key, 6)
    fast_share = 4
    fast_heads = jax.random.randint(key_rows[0], (VALUE_HEADS, 1), 0, 8) < fast_share
    spans = jax.random.uniform(key_rows[1], (VALUE_HEADS, 1), minval=30.0, maxval=50.0)
    slow_total = jax.random.uniform(key_rows[2], (VALUE_HEADS, 1), minval=0.1, maxval=0.5)
    starting_rate = jnp.where(fast_heads, 1.0 / spans, slow_total / TOKEN_COUNT)
    noise_level = jnp.exp(jax.random.uniform(key_rows[3], (VALUE_HEADS, TOKEN_COUNT), minval=-0.7, maxval=0.7))
    places = jax.random.randint(key_rows[4], (VALUE_HEADS, 3, 1), 0, TOKEN_COUNT)
    query_matches = jnp.sum((jnp.arange(TOKEN_COUNT)[None, None, :] == places).astype(jnp.float32), axis=1)
    position_groups = jnp.log(jax.random.uniform(key_rows[5], (VALUE_HEADS, TOKEN_COUNT), minval=0.6, maxval=0.8))
    return (-starting_rate * noise_level + query_matches * position_groups).astype(jnp.float32)


def steps_of(own_key, dims, pieces, low, largest):
    gain = 1.0
    for dim, shards_of in pieces:
        draws = jax.random.uniform(jax.random.fold_in(jax.random.fold_in(own_key, 6), dim), (shards_of,), jnp.float32, low / len(pieces), largest / len(pieces))
        gain = gain * jnp.repeat(jnp.exp(draws), dims[dim] // shards_of).reshape((-1,) + (1,) * (len(dims) - 1 - dim))
    return gain


def normal_values(rng, dims, deviation, most, shards=(), held_as=jnp.bfloat16):
    gain = steps_of(rng, dims, shards, -0.22, 0.18) if shards else 1.0
    result = jax.random.normal(rng, dims, jnp.float32) * deviation * gain
    return jnp.minimum(jnp.maximum(result, -most), most).astype(held_as)


def setup_inputs(seed: int = 0, part: int = 0) -> dict:
    key_of = jax.random.split(jax.random.key(seed), 10)
    part_keys = jax.random.split(jax.random.fold_in(key_of[9], part), 10)
    query = draw_query(jax.random.fold_in(jax.random.fold_in(key_of[9], part), 71), part)
    key = draw_key(jax.random.fold_in(jax.random.fold_in(key_of[9], part), 71), part)
    value = normal_values(part_keys[2], (TOKEN_COUNT, VALUE_HEADS * HD), 1.0, 6.0, ((0, 32), (1, 4)))
    out_grad = normal_values(part_keys[3], (TOKEN_COUNT, VALUE_HEADS * HD), 1.0, 6.0, ((0, 32), (1, 4)))
    log_decay = draw_log_decay(jax.random.fold_in(jax.random.fold_in(key_of[9], part), 71), part)
    beta = jnp.clip(0.05 + 0.9 * jax.random.uniform(part_keys[5], (VALUE_HEADS, TOKEN_COUNT), jnp.float32) ** steps_of(part_keys[5], (VALUE_HEADS, TOKEN_COUNT), ((0, 4), (1, 32)), -0.2, 0.2), 0.05, 0.95)
    w_query = normal_values(key_of[6], (D, NK * HD), D ** -0.5, 0.125, ((1, 4),))
    w_key = normal_values(key_of[7], (D, NK * HD), D ** -0.5, 0.125, ((1, 4),))
    w_value = normal_values(key_of[8], (D, VALUE_HEADS * HD), D ** -0.5, 0.125, ((1, 4),))
    return dict(query=query, key=key, value=value, out_grad=out_grad, log_decay=log_decay, beta=beta, w_query=w_query, w_key=w_key, w_value=w_value)


accurate_arithmetic_mode = lax.Precision.HIGHEST

def unit_rows(values):
    return values * lax.rsqrt(lax.optimization_barrier(jnp.sum(values * values, axis=-1, keepdims=True)) + 1e-06)

def token_step(memory_state, inputs):
    query_normalized, key_normalized, value_row, gate, rate = inputs
    decay = jnp.exp(gate)
    recalled_values = jnp.einsum('zs,zsm->zm', key_normalized, memory_state, precision=accurate_arithmetic_mode)
    update = rate[:, None] * (value_row - decay[:, None] * recalled_values)
    memory_state = decay[:, None, None] * memory_state + key_normalized[:, :, None] * update[:, None, :]
    return (memory_state, jnp.einsum('zs,zsm->zm', query_normalized, memory_state, precision=accurate_arithmetic_mode))

def block_rows(array):
    return array.reshape((TOKEN_COUNT // STRETCH, STRETCH) + array.shape[1:])

def forward(query, key, value, log_decay, beta):
    repeat = VALUE_HEADS // NK
    query_normalized = jnp.repeat(unit_rows(query.reshape(TOKEN_COUNT, NK, HD)) * HD ** (-0.5), repeat, axis=1)
    key_normalized = jnp.repeat(unit_rows(key.reshape(TOKEN_COUNT, NK, HD)), repeat, axis=1)
    value_rows = value.reshape(TOKEN_COUNT, VALUE_HEADS, HD)
    inputs = (query_normalized, key_normalized, value_rows, log_decay.T, beta.T)
    blocked = jax.tree.map(block_rows, inputs)
    run_block = jax.checkpoint(partial(lax.scan, token_step))

    def outer_step(memory_state, block_inputs):
        return run_block(memory_state, block_inputs)
    final_state, outputs = lax.scan(outer_step, jnp.zeros((VALUE_HEADS, HD, HD), jnp.float32), blocked)
    return outputs.reshape(TOKEN_COUNT, VALUE_HEADS * HD)

def reference(query, key, value, out_grad, log_decay, beta, w_query, w_key, w_value):
    outputs, pull = jax.vjp(forward, query.astype(jnp.float32), key.astype(jnp.float32), value.astype(jnp.float32), log_decay, beta)
    grad_query, derivative_lookup_vector, grad_value, decay_grad, beta_grad = pull(out_grad.astype(jnp.float32))
    input_grad = jnp.dot(grad_query.astype(jnp.bfloat16), w_query.T, preferred_element_type=jnp.float32)
    input_grad = input_grad + jnp.dot(derivative_lookup_vector.astype(jnp.bfloat16), w_key.T, preferred_element_type=jnp.float32)
    input_grad = input_grad + jnp.dot(grad_value.astype(jnp.bfloat16), w_value.T, preferred_element_type=jnp.float32)
    return (input_grad.astype(jnp.bfloat16), decay_grad, beta_grad)
```

```python
import functools

import jax
import jax.numpy as jnp
from jax import lax
from jax.experimental import pallas as pl
from jax.experimental.pallas import tpu as pltpu
from jax.sharding import PartitionSpec as P

MESH = pl.DeviceIdType.MESH
f32 = jnp.float32
bf16 = jnp.bfloat16
HD = 128
NY = 4
PAIR = 2
NN = (((1,), (0,)), ((), ()))
NT = (((1,), (1,)), ((), ()))
TN = (((0,), (0,)), ((), ()))


def split(x, n=2):
    if isinstance(x, (list, tuple)):
        return x
    if x.dtype == bf16:
        return [x]
    out = []
    for _ in range(n - 1):
        h = x.astype(bf16)
        out.append(h)
        x = x - h.astype(f32)
    out.append(x.astype(bf16))
    return out


def mm(a, b, dims=NN, n=2):
    a, b = split(a, n), split(b, n)
    total = None
    for i in reversed(range(len(a))):
        for j in reversed(range(len(b))):
            if i + j < n:
                term = lax.dot_general(a[i], b[j], dims, preferred_element_type=f32)
                total = term if total is None else total + term
    return total


def iotas(n):
    i = lax.broadcasted_iota(jnp.int32, (n, n), 0)
    j = lax.broadcasted_iota(jnp.int32, (n, n), 1)
    return i, j


def lower_inverses(blocks):
    n = HD
    i, j = iotas(n)
    eye = jnp.where(i == j, 1.0, 0.0).astype(f32)
    apart = i ^ j
    xs = [eye - jnp.where(apart == 1, b, 0.0) for b in blocks]
    level = 1
    while (1 << level) < n:
        here = (apart >> level) == 1
        xb = [x.astype(bf16) for x in xs]
        ys = [mm(jnp.where(here, b, 0.0).astype(bf16), x) for b, x in zip(blocks, xb)]
        xs = [x - mm(h, y.astype(bf16)) for x, h, y in zip(xs, xb, ys)]
        level += 1
    sp = [split(x) for x in xs]
    rs = [eye - x - mm(b, s) for b, x, s in zip(blocks, xs, sp)]
    return [x + mm(s, r) for x, s, r in zip(xs, sp, rs)]


def kernel(
    nx, groups,
    q_ref, k_ref, v_ref, do_ref, ld_ref, be_ref, wq_hbm, wk_hbm, wv_hbm,
    ig_ref, dld_ref, dbe_ref,
    wq, wk, wv,
    qs, ks, qn, kn, gam, th, tl, ub, wm, duo,
    snd1, rcv1, snd2, rcv2, st, snd3, rcv3,
    gbuf, pd2, pr, pl_, r2, rin,
    wsem, s1, v1, s2, v2, s3, v3, s4, v4,
):
    rows = q_ref.shape[0]
    heads = ld_ref.shape[0]
    kheads = q_ref.shape[1] // HD
    rep = heads // kheads
    ctx = lax.axis_index("ctx")
    me = lax.axis_index("head")
    z, y = ctx // NY, ctx % NY
    zg, kind = z // PAIR, z % PAIR
    cpg = PAIR * NY
    here = kind * NY + y
    pos = zg + kind * (groups - 1 - 2 * zg)
    up, down = (me + 1) % nx, (me + nx - 1) % nx

    def at(zz, yy):
        return {"ctx": zz * NY + yy}

    barrier = pltpu.get_barrier_semaphore()
    for d in range(1, cpg):
        c = (here + d) % cpg
        pl.semaphore_signal(barrier, inc=1, device_id=at(zg * PAIR + c // NY, c % NY), device_id_type=MESH)
    for d in range(1, groups):
        g = (zg + d) % groups
        pl.semaphore_signal(barrier, inc=1, device_id=at(g * PAIR + kind, y), device_id_type=MESH)
    for n in (up, down):
        pl.semaphore_signal(barrier, inc=1, device_id={"head": n}, device_id_type=MESH)

    loads = [
        pltpu.make_async_copy(a, b, wsem.at[i])
        for i, (a, b) in enumerate(((wq_hbm, wq), (wk_hbm, wk), (wv_hbm, wv)))
    ]
    for load in loads:
        load.start()

    i, j = iotas(rows)
    lower, strict = i >= j, i > j
    tri = jnp.where(lower, 1.0, 0.0).astype(bf16)
    unit = jnp.where(i == j, 1.0, 0.0).astype(bf16)
    ld = jnp.concatenate([ld_ref[...]] * 4, axis=0)
    be = jnp.concatenate([be_ref[...]] * 4, axis=0)
    lds = split(ld, 3)
    c_cols = mm(tri, lds, NT, 3)
    c_rows = mm(lds, tri, NT, 3)
    b_cols = mm(unit, split(be, 3), NT, 3)
    c_col = [c_cols[:, h : h + 1] for h in range(heads)]
    b_col = [b_cols[:, h : h + 1] for h in range(heads)]
    gamma = [jnp.exp(c) for c in c_col]
    c_end = [c[rows - 1 :, :] for c in c_col]
    gend = [jnp.exp(e - c) for e, c in zip(c_end, c_col)]

    i1, j1 = iotas(HD)
    eye = jnp.where(i1 == j1, 1.0, 0.0).astype(f32)

    scale = HD**-0.5
    kk, qk = [], []
    for g in range(kheads):
        cols = slice(g * HD, (g + 1) * HD)
        qf, kf = q_ref[:, cols].astype(f32), k_ref[:, cols].astype(f32)
        rq = lax.rsqrt(jnp.sum(qf * qf, axis=1, keepdims=True) + 1e-6)
        rk = lax.rsqrt(jnp.sum(kf * kf, axis=1, keepdims=True) + 1e-6)
        qu, ku = qf * rq, kf * rk
        qn[g], kn[g] = qu, ku
        qsp, ksp = split(qu * scale), split(ku)
        for t in range(2):
            qs[g, t], ks[g, t] = qsp[t], ksp[t]
        kk.append(mm(ksp, ksp, NT))
        qk.append(mm(qsp, ksp, NT))

    blocks, corners = [], []
    mix = []
    for h in range(heads):
        w = jnp.where(lower, jnp.exp(jnp.minimum(c_col[h] - c_rows[h : h + 1, :], 0.0)), 0.0)
        gam[h] = w
        low = jnp.where(strict, w * kk[h // rep], 0.0) * b_col[h]
        mix.append(split(w * qk[h // rep]))
        blocks += [low[:HD, :HD], low[HD:, HD:]]
        corners.append(low[HD:, :HD])
    inv = [split(x) for x in lower_inverses(blocks)]
    mids = [mm(corners[h], inv[2 * h]) for h in range(heads)]
    inv21 = [split(-mm(inv[2 * h + 1], mids[h])) for h in range(heads)]
    zero = jnp.zeros((HD, HD), bf16)
    for h in range(heads):
        for t, ref in enumerate((th, tl)):
            ref[h, :HD, :HD] = inv[2 * h][t]
            ref[h, :HD, HD:] = zero
            ref[h, HD:, :HD] = inv21[h][t]
            ref[h, HD:, HD:] = inv[2 * h + 1][t]

    def head(ref, h):
        return ref[:, h * HD : (h + 1) * HD]

    def send1(h, kk_):
        slot = here + kk_ * (cpg - 1 - 2 * here)
        return pltpu.make_async_remote_copy(
            src_ref=snd1.at[h, kk_], dst_ref=rcv1.at[slot],
            send_sem=s1.at[h, kk_], recv_sem=v1.at[slot],
            device_id=at(zg * PAIR + kk_, h), device_id_type=MESH,
        )

    def mine(h, kk_):
        return (y == h) & (kind == kk_)

    def dispatch(h, kk_):
        slot = here + kk_ * (cpg - 1 - 2 * here)

        @pl.when(mine(h, kk_))
        def _():
            rcv1[slot] = snd1[h, kk_]

        @pl.when(jnp.logical_not(mine(h, kk_)))
        def _():
            send1(h, kk_).start()

    for h in range(heads):
        g = h // rep
        ksp = (ks[g, 0], ks[g, 1])
        ku, qu = kn[g], qn[g]
        tsp = (th[h], tl[h])
        right = jnp.concatenate([b_col[h] * head(v_ref, h).astype(f32), (b_col[h] * gamma[h]) * ku], axis=1)
        uw = mm(tsp, right)
        ub[h], wm[h] = uw[:, :HD], uw[:, HD:]
        uws = split(uw)
        kend = split(gend[h] * ku)
        ba = mm(kend, uws, TN)
        a = jnp.exp(c_end[h]) * eye - ba[:, HD:]
        snd1[h, 0, 0] = a
        snd1[h, 0, 1] = ba[:, :HD]
        snd1[h, 1, 0] = a.T
        d = mm(mix[h], head(do_ref, h), TN)
        duo[h] = d
        wsp = [t[:, HD:] for t in uws]
        snd1[h, 1, 1] = mm((gamma[h] * scale) * qu, head(do_ref, h), TN) - mm(wsp, d, TN)

    pl.semaphore_wait(barrier, cpg + groups)
    for h in range(heads):
        for kk_ in range(PAIR):
            dispatch(h, kk_)

    def wait1(s):
        @pl.when(s != here + kind * (cpg - 1 - 2 * here))
        def _():
            pltpu.make_async_remote_copy(
                src_ref=snd1.at[0, 0], dst_ref=rcv1.at[s], send_sem=s1.at[0, 0], recv_sem=v1.at[s],
                device_id=at(z, y), device_id_type=MESH,
            ).wait_recv()

    for s in range(cpg):
        wait1(s)

    def after(second, first):
        (a2, b2), (a1, b1) = second, first
        r = mm(a2, jnp.concatenate([a1, b1], axis=1))
        return r[:, :HD], r[:, HD:] + b2

    maps = [(rcv1[s, 0], rcv1[s, 1]) for s in range(cpg)]
    two = [after(maps[2 * t + 1], maps[2 * t]) for t in range(cpg // 2)]
    four = [after(two[1], two[0]), after(two[3], two[2])]
    whole = after(four[1], four[0])
    snd2[0], snd2[1] = whole

    def send2(src, dst):
        gg = dst + kind * (groups - 1 - 2 * dst)
        lo = 1 if src == 0 else 0
        return pltpu.make_async_remote_copy(
            src_ref=snd2.at[lo:], dst_ref=rcv2.at[src, lo:],
            send_sem=s2.at[dst], recv_sem=v2.at[src],
            device_id=at(gg * PAIR + kind, y), device_id_type=MESH,
        )

    for src in range(groups - 1):
        @pl.when(pos == src)
        def _():
            for dst in reversed(range(src + 1, groups)):
                send2(src, dst).start()

    pre = [maps[0], two[0], after(maps[2], two[0]), four[0]]
    pre += [after(maps[4], four[0]), after(two[2], four[0])]
    pre.append(after(maps[6], pre[5]))

    st[...] = jnp.zeros_like(st)
    for dst in range(1, groups):
        @pl.when(pos == dst)
        def _():
            for src in range(dst):
                send2(src, dst).wait_recv()
            state = rcv2[0, 1]
            for src in range(1, dst):
                state = mm(rcv2[src, 0], state) + rcv2[src, 1]
            st[...] = state

    state = st[...]
    ssp = split(state)
    snd3[0] = state
    for s in range(1, cpg):
        a, b = pre[s - 1]
        snd3[s] = mm(a, ssp) + b

    def send3(d):
        c = (here + d) % cpg
        s = c + kind * (cpg - 1 - 2 * c)
        return pltpu.make_async_remote_copy(
            src_ref=snd3.at[s], dst_ref=rcv3.at[y, kind],
            send_sem=s3.at[d], recv_sem=v3.at[y, kind],
            device_id=at(zg * PAIR + c // NY, c % NY), device_id_type=MESH,
        )

    for d in range(1, cpg):
        send3(d).start()
    rcv3[y, kind] = snd3[here + kind * (cpg - 1 - 2 * here)]

    def wait3(h, kk_):
        @pl.when(jnp.logical_not(mine(h, kk_)))
        def _():
            pltpu.make_async_remote_copy(
                src_ref=snd3.at[0], dst_ref=rcv3.at[h, kk_], send_sem=s3.at[0], recv_sem=v3.at[h, kk_],
                device_id=at(z, y), device_id_type=MESH,
            ).wait_recv()

    for h in range(heads):
        for kk_ in range(PAIR):
            wait3(h, kk_)

    ones = jnp.ones((16, HD), bf16)
    for g in range(kheads):
        ku, qu = kn[g], qn[g]
        ksp, qsp = (ks[g, 0], ks[g, 1]), (qs[g, 0], qs[g, 1])
        qhat = qu * scale
        dq_sum = dk_sum = None
        for h in range(g * rep, (g + 1) * rep):
            s, c = rcv3[h, 0], rcv3[h, 1]
            ssp, csp = split(s), split(c)
            w, do = gam[h], head(do_ref, h)
            kend = gend[h] * ku
            u = ub[h] - mm(wm[h], ssp)
            usp = split(u)
            du = duo[h] + mm(kend, csp)
            dr = mm((th[h], tl[h]), du, TN)
            rsp = split(dr)
            dm = split(mm(do, usp, NT) * w)
            dl = split(jnp.where(strict, -(mm(rsp, usp, NT) * w), 0.0))
            dq = mm(dm, ksp) + gamma[h] * mm(do, ssp, NT)
            e = mm(dl, ksp) - gamma[h] * mm(rsp, ssp, NT)
            ug = gend[h] * mm(usp, csp, NT)
            dkw = mm(dm, qsp, TN) + mm(dl, b_col[h] * ku, TN) + ug
            left = b_col[h] * e
            dk = left + dkw
            gbuf[:, (2 * kheads + h) * HD : (2 * kheads + h + 1) * HD] = (b_col[h] * dr).astype(bf16)
            rate = mm(ones, dr * head(v_ref, h).astype(f32) + ku * e, NT, 3)
            dbe_ref[h : h + 1, :] = rate[:1, :]
            dcum = mm(ones, qhat * dq + ku * (left - dkw), NT, 3)
            ends = jnp.sum(ku * ug, axis=0, keepdims=True) + jnp.exp(c_end[h]) * jnp.sum(c * s, axis=0, keepdims=True)
            dld = mm(dcum, tri, NN, 3) + jnp.sum(ends, axis=1, keepdims=True)
            dld_ref[h : h + 1, :] = dld[:1, :]
            dq_sum = dq if dq_sum is None else dq_sum + dq
            dk_sum = dk if dk_sum is None else dk_sum + dk
        for x_ref, unit_rows, grad, at_col, mult in (
            (q_ref, qu, dq_sum, g, scale), (k_ref, ku, dk_sum, kheads + g, 1.0),
        ):
            xf = x_ref[:, g * HD : (g + 1) * HD].astype(f32)
            r = lax.rsqrt(jnp.sum(xf * xf, axis=1, keepdims=True) + 1e-6) * mult
            out = r * (grad - unit_rows * jnp.sum(unit_rows * grad, axis=1, keepdims=True))
            gbuf[:, at_col * HD : (at_col + 1) * HD] = out.astype(bf16)

    for load in loads:
        load.wait()
    part = rows // nx
    half = wq.shape[0] // 2
    kw = kheads * HD

    def project(dest, side):
        grads = gbuf[pl.ds(pl.multiple_of(dest * part, part), part), :]
        outs = slice(side * half, (side + 1) * half)
        total = lax.dot_general(grads[:, :kw], wq[outs, :], NT, preferred_element_type=f32)
        total += lax.dot_general(grads[:, kw : 2 * kw], wk[outs, :], NT, preferred_element_type=f32)
        total += lax.dot_general(grads[:, 2 * kw :], wv[outs, :], NT, preferred_element_type=f32)
        return total

    def hop(src, dst, n, to):
        return pltpu.make_async_remote_copy(
            src_ref=src, dst_ref=dst, send_sem=s4.at[n], recv_sem=v4.at[n],
            device_id={"head": to}, device_id_type=MESH,
        )

    hops = [
        hop(pd2.at[0], r2.at[0], 0, up), hop(pd2.at[1], r2.at[1], 1, down),
        hop(pr.at[1], rin.at[0, 1], 2, up), hop(pl_.at[0], rin.at[1, 0], 3, down),
        hop(pr.at[0], rin.at[0, 0], 4, up), hop(pl_.at[1], rin.at[1, 1], 5, down),
    ]
    far = (me + 2) % nx
    pd2[0] = project(far, 0)
    hops[0].start()
    pd2[1] = project(far, 1)
    hops[1].start()
    pr[1] = project(up, 1)
    hops[2].start()
    pl_[0] = project(down, 0)
    hops[3].start()
    pr[0] = project(up, 0)
    pl_[1] = project(down, 1)
    hops[0].wait_recv()
    pr[0] = pr[0] + r2[0]
    hops[4].start()
    hops[1].wait_recv()
    pl_[1] = pl_[1] + r2[1]
    hops[5].start()
    own = [project(me, 0), project(me, 1)]
    for n in (2, 3, 4, 5):
        hops[n].wait_recv()
    for side in range(2):
        total = own[side] + rin[0, side] + rin[1, side]
        ig_ref[:, side * half : (side + 1) * half] = total.astype(bf16)

    for n in range(6):
        hops[n].wait_send()
    for d in range(1, cpg):
        send3(d).wait_send()
    for src in range(groups - 1):
        @pl.when(pos == src)
        def _():
            for dst in range(src + 1, groups):
                send2(src, dst).wait_send()
    for h in range(heads):
        for kk_ in range(PAIR):
            @pl.when(jnp.logical_not(mine(h, kk_)))
            def _():
                send1(h, kk_).wait_send()


def solution(mesh):
    nx = mesh.shape["head"]
    groups = mesh.shape["ctx"] // (NY * PAIR)

    def per_device(q, k, v, do, ld, be, wq, wk, wv):
        rows, heads = q.shape[0], ld.shape[0]
        kheads = q.shape[1] // HD
        model = wq.shape[0]
        part, half = rows // nx, model // 2
        cpg = PAIR * NY
        vmem = pl.BlockSpec(memory_space=pltpu.VMEM)
        hbm = pl.BlockSpec(memory_space=pl.ANY)

        def buf(*shape, dtype=f32):
            return pltpu.VMEM(shape, dtype)

        dma = pltpu.SemaphoreType.DMA
        scratch = [
            buf(*wq.shape, dtype=bf16), buf(*wk.shape, dtype=bf16), buf(*wv.shape, dtype=bf16),
            buf(kheads, 2, rows, HD, dtype=bf16), buf(kheads, 2, rows, HD, dtype=bf16),
            buf(kheads, rows, HD), buf(kheads, rows, HD),
            buf(heads, rows, rows),
            buf(heads, rows, rows, dtype=bf16), buf(heads, rows, rows, dtype=bf16),
            buf(heads, rows, HD), buf(heads, rows, HD), buf(heads, rows, HD),
            buf(heads, PAIR, 2, HD, HD), buf(cpg, 2, HD, HD),
            buf(2, HD, HD), buf(groups - 1, 2, HD, HD), buf(HD, HD),
            buf(cpg, HD, HD), buf(heads, PAIR, HD, HD),
            buf(rows, (2 * kheads + heads) * HD, dtype=bf16),
            buf(2, part, half), buf(2, part, half), buf(2, part, half),
            buf(2, part, half), buf(2, 2, part, half),
            dma((3,)), dma((heads, PAIR)), dma((cpg,)), dma((groups,)), dma((groups,)),
            dma((cpg,)), dma((heads, PAIR)), dma((6,)), dma((6,)),
        ]
        return pl.pallas_call(
            functools.partial(kernel, nx, groups),
            out_shape=(
                jax.ShapeDtypeStruct((part, model), bf16),
                jax.ShapeDtypeStruct(ld.shape, f32),
                jax.ShapeDtypeStruct(be.shape, f32),
            ),
            in_specs=[vmem] * 6 + [hbm] * 3,
            out_specs=(vmem, vmem, vmem),
            scratch_shapes=scratch,
            compiler_params=pltpu.CompilerParams(
                collective_id=0, has_side_effects=True, vmem_limit_bytes=56 << 20
            ),
            name="delta_backward",
        )(q, k, v, do, ld, be, wq, wk, wv)

    row = P(("dp", "ctx"), "head")
    gate = P("head", ("dp", "ctx"))
    weight = P(None, "head")
    return jax.shard_map(
        per_device, mesh=mesh,
        in_specs=(row, row, row, row, gate, gate, weight, weight, weight),
        out_specs=(P(("dp", "ctx", "head"), None), gate, gate),
        check_vma=False,
    )
```

```python
import functools

import jax
import jax.numpy as jnp
from jax import lax
from jax.experimental import pallas as pl
from jax.experimental.pallas import tpu as pltpu
from jax.sharding import PartitionSpec as P

MESH = pl.DeviceIdType.MESH
f32 = jnp.float32
bf16 = jnp.bfloat16
HD = 128
NY = 4
PAIR = 2
NN = (((1,), (0,)), ((), ()))
NT = (((1,), (1,)), ((), ()))
TN = (((0,), (0,)), ((), ()))


def split(x, n=2):
    if isinstance(x, (list, tuple)):
        return x
    if x.dtype == bf16:
        return [x]
    out = []
    for _ in range(n - 1):
        h = x.astype(bf16)
        out.append(h)
        x = x - h.astype(f32)
    out.append(x.astype(bf16))
    return out


def mm(a, b, dims=NN, n=2):
    a, b = split(a, n), split(b, n)
    total = None
    for i in reversed(range(len(a))):
        for j in reversed(range(len(b))):
            if i + j < n:
                term = lax.dot_general(a[i], b[j], dims, preferred_element_type=f32)
                total = term if total is None else total + term
    return total


def iotas(n):
    i = lax.broadcasted_iota(jnp.int32, (n, n), 0)
    j = lax.broadcasted_iota(jnp.int32, (n, n), 1)
    return i, j


def lower_inverses(blocks):
    n = HD
    i, j = iotas(n)
    eye = jnp.where(i == j, 1.0, 0.0).astype(f32)
    apart = i ^ j
    xs = [eye - jnp.where(apart == 1, b, 0.0) for b in blocks]
    level = 1
    while (1 << level) < n:
        here = (apart >> level) == 1
        xb = [x.astype(bf16) for x in xs]
        ys = [mm(jnp.where(here, b, 0.0).astype(bf16), x) for b, x in zip(blocks, xb)]
        xs = [x - mm(h, y.astype(bf16)) for x, h, y in zip(xs, xb, ys)]
        level += 1
    sp = [split(x) for x in xs]
    rs = [eye - x - mm(b, s) for b, x, s in zip(blocks, xs, sp)]
    return [x + mm(s, r) for x, s, r in zip(xs, sp, rs)]


def kernel(
    nx, groups,
    q_ref, k_ref, v_ref, do_ref, ld_ref, be_ref, wq_hbm, wk_hbm, wv_hbm,
    ig_ref, dld_ref, dbe_ref,
    wq, wk, wv,
    qs, ks, qn, kn, kkb, qkb, gam, gamt, low_, lowt, ub, wm, ke, xr, yr, us, rs,
    bcol, gcol, ecol, ebeta, ecum,
    snd1, rcv1, snd2, rcv2, st, pre_, snd3, rcv3,
    gbuf, pd2, pr, pl_, r2, rin,
    wsem, s1, v1, s2, v2, s3, v3, s4, v4,
):
    rows = q_ref.shape[0]
    heads = ld_ref.shape[0]
    kheads = q_ref.shape[1] // HD
    rep = heads // kheads
    ctx = lax.axis_index("ctx")
    me = lax.axis_index("head")
    z, y = ctx // NY, ctx % NY
    zg, kind = z // PAIR, z % PAIR
    cpg = PAIR * NY
    here = kind * NY + y
    pos = zg + kind * (groups - 1 - 2 * zg)
    up, down = (me + 1) % nx, (me + nx - 1) % nx

    def at(zz, yy):
        return {"ctx": zz * NY + yy}

    barrier = pltpu.get_barrier_semaphore()
    for d in range(1, cpg):
        c = (here + d) % cpg
        pl.semaphore_signal(barrier, inc=1, device_id=at(zg * PAIR + c // NY, c % NY), device_id_type=MESH)
    for d in range(1, groups):
        g = (zg + d) % groups
        pl.semaphore_signal(barrier, inc=1, device_id=at(g * PAIR + kind, y), device_id_type=MESH)
    for n in (up, down):
        pl.semaphore_signal(barrier, inc=1, device_id={"head": n}, device_id_type=MESH)

    loads = [
        pltpu.make_async_copy(a, b, wsem.at[i])
        for i, (a, b) in enumerate(((wq_hbm, wq), (wk_hbm, wk), (wv_hbm, wv)))
    ]
    for load in loads:
        load.start()

    order = (2, 1, 3, 0)
    i, j = iotas(rows)
    lower, strict = i >= j, i > j
    tri = jnp.where(lower, 1.0, 0.0).astype(bf16)
    unit = jnp.where(i == j, 1.0, 0.0).astype(bf16)

    def own_head(d):
        return (y + d) % NY

    def turned(ref):
        turn = [ref[pl.ds(own_head(d), 1), :] for d in range(heads)]
        return split(jnp.concatenate(turn * 4, axis=0), 3)

    lds = turned(ld_ref)
    c_cols = mm(tri, lds, NT, 3)
    c_rows = mm(lds, tri, NT, 3)
    b_cols = mm(unit, turned(be_ref), NT, 3)
    c_col = [c_cols[:, d : d + 1] for d in range(heads)]
    b_col = [b_cols[:, d : d + 1] for d in range(heads)]
    gamma = [jnp.exp(c) for c in c_col]
    c_end = [c[rows - 1 :, :] for c in c_col]
    gend = [jnp.exp(e - c) for e, c in zip(c_end, c_col)]

    i1, j1 = iotas(HD)
    eye = jnp.where(i1 == j1, 1.0, 0.0).astype(f32)

    scale = HD**-0.5
    for g in range(kheads):
        cols = slice(g * HD, (g + 1) * HD)
        qf, kf = q_ref[:, cols].astype(f32), k_ref[:, cols].astype(f32)
        rq = lax.rsqrt(jnp.sum(qf * qf, axis=1, keepdims=True) + 1e-6)
        rk = lax.rsqrt(jnp.sum(kf * kf, axis=1, keepdims=True) + 1e-6)
        qu, ku = qf * rq, kf * rk
        qn[g], kn[g] = qu, ku
        qsp, ksp = split(qu * scale), split(ku)
        for t in range(2):
            qs[g, t], ks[g, t] = qsp[t], ksp[t]
        kkb[g] = mm(ksp, ksp, NT)
        qkb[g] = mm(qsp, ksp, NT)

    def head(ref, h):
        return ref[:, h * HD : (h + 1) * HD]

    def turned_head(ref, d):
        return ref[:, pl.ds(pl.multiple_of(own_head(d) * HD, HD), HD)]

    def slot_of(c, kk_):
        return c + kk_ * (cpg - 1 - 2 * c)

    def send1(d, kk_):
        slot = slot_of(here, kk_)
        return pltpu.make_async_remote_copy(
            src_ref=snd1.at[d, kk_], dst_ref=rcv1.at[slot],
            send_sem=s1.at[d, kk_], recv_sem=v1.at[slot],
            device_id=at(zg * PAIR + kk_, own_head(d)), device_id_type=MESH,
        )

    sends1 = [send1(d, kk_) for d in order[:-1] for kk_ in range(PAIR)] + [send1(0, 1 - kind)]

    zero = jnp.zeros((HD, HD), bf16)
    tsps, duos = {}, {}
    for pair in (order,):
        blocks, corners, mix = [], [], []
        for d in pair:
            g = own_head(d) // rep
            w = jnp.where(lower, jnp.exp(jnp.minimum(c_col[d] - c_rows[d : d + 1, :], 0.0)), 0.0)
            gam[d] = w
            low = jnp.where(strict, w * kkb[g], 0.0) * b_col[d]
            mix.append(split(w * qkb[g]))
            blocks += [low[:HD, :HD], low[HD:, HD:]]
            corners.append(low[HD:, :HD])
        inv = [split(x) for x in lower_inverses(blocks)]
        mids = [mm(c, inv[2 * n]) for n, c in enumerate(corners)]
        inv21 = [split(-mm(inv[2 * n + 1], m)) for n, m in enumerate(mids)]
        for n, d in enumerate(pair):
            tsp = [
                jnp.concatenate(
                    [
                        jnp.concatenate([inv[2 * n][t], zero], axis=1),
                        jnp.concatenate([inv21[n][t], inv[2 * n + 1][t]], axis=1),
                    ],
                    axis=0,
                )
                for t in range(2)
            ]
            g = own_head(d) // rep
            ku, qu = kn[g], qn[g]
            do = turned_head(do_ref, d)
            right = jnp.concatenate([b_col[d] * turned_head(v_ref, d).astype(f32), (b_col[d] * gamma[d]) * ku], axis=1)
            uw = mm(tsp, right)
            ub[d] = uw[:, :HD]
            uws = split(uw)
            kend = split(gend[d] * ku)
            wsp = [t[:, HD:] for t in uws]
            for t in range(2):
                wm[d, t], ke[d, t] = wsp[t], kend[t]
            ba = mm(kend, uws, TN)
            a = jnp.exp(c_end[d]) * eye - ba[:, HD:]
            snd1[d, 0, 0] = a
            snd1[d, 0, 1] = ba[:, :HD]
            snd1[d, 1, 0] = a.T
            duo = mm(mix[n], do, TN)
            snd1[d, 1, 1] = mm((gamma[d] * scale) * qu, do, TN) - mm(wsp, duo, TN)
            tsps[d], duos[d] = tsp, duo
            if n == 0:
                pl.semaphore_wait(barrier, cpg + groups)
            for copy in sends1[PAIR * n : PAIR * (n + 1)]:
                copy.start()
    rcv1[slot_of(here, kind)] = snd1[0, kind]

    for d in range(heads):
        xr[d] = mm(tsps[d], duos[d], TN)
        ysp = split(mm(tsps[d], (ke[d, 0], ke[d, 1]), TN))
        for t in range(2):
            yr[d, t] = ysp[t]
        w = gam[d]
        wt = jnp.where(i <= j, jnp.exp(jnp.minimum(c_rows[d : d + 1, :] - c_col[d], 0.0)), 0.0)
        gamt[d] = wt
        low_[d] = jnp.where(strict, -w, 0.0)
        lowt[d] = jnp.where(i < j, -wt, 0.0)
    c_cols = mm(tri, split(jnp.concatenate([ld_ref[...]] * 4, axis=0), 3), NT, 3)
    bcol[...] = mm(unit, split(jnp.concatenate([be_ref[...]] * 4, axis=0), 3), NT, 3)
    gcol[...] = jnp.exp(c_cols)
    ecol[...] = jnp.exp(c_cols[rows - 1 :, :] - c_cols)
    whole_decay = jnp.exp(c_cols[rows - 1 :, :])

    for d in range(1, cpg):
        s = slot_of((here + d) % cpg, kind)
        pltpu.make_async_remote_copy(
            src_ref=snd1.at[0, 0], dst_ref=rcv1.at[s], send_sem=s1.at[0, 0], recv_sem=v1.at[s],
            device_id=at(z, y), device_id_type=MESH,
        ).wait_recv()

    def after(second, first):
        (a2, b2), (a1, b1) = second, first
        r = mm(a2, jnp.concatenate([a1, b1], axis=1))
        return r[:, :HD], r[:, HD:] + b2

    maps = [(rcv1[s, 0], rcv1[s, 1]) for s in range(cpg)]
    two = [after(maps[2 * t + 1], maps[2 * t]) for t in range(cpg // 2)]
    four = [after(two[1], two[0]), after(two[3], two[2])]
    whole = after(four[1], four[0])
    snd2[0], snd2[1] = whole

    def send2(src, dst):
        gg = dst + kind * (groups - 1 - 2 * dst)
        lo = 1 if src == 0 else 0
        return pltpu.make_async_remote_copy(
            src_ref=snd2.at[lo:], dst_ref=rcv2.at[src, lo:],
            send_sem=s2.at[dst], recv_sem=v2.at[src],
            device_id=at(gg * PAIR + kind, y), device_id_type=MESH,
        )

    for src in range(groups - 1):
        @pl.when(pos == src)
        def _():
            for dst in reversed(range(src + 1, groups)):
                send2(src, dst).start()

    pre = [maps[0], two[0], after(maps[2], two[0]), four[0]]
    pre += [after(maps[4], four[0]), after(two[2], four[0])]
    pre.append(after(maps[6], pre[5]))

    pre_[0, 0] = eye
    pre_[0, 1] = jnp.zeros((HD, HD), f32)
    for n, (a, b) in enumerate(pre):
        pre_[n + 1, 0], pre_[n + 1, 1] = a, b

    st[...] = jnp.zeros_like(st)
    for dst in range(1, groups):
        @pl.when(pos == dst)
        def _():
            for src in range(dst):
                send2(src, dst).wait_recv()
            state = rcv2[0, 1]
            for src in range(1, dst):
                state = mm(rcv2[src, 0], state) + rcv2[src, 1]
            st[...] = state

    ssp = split(st[...])

    def send3(d):
        c = (here + d) % cpg
        return pltpu.make_async_remote_copy(
            src_ref=snd3.at[d], dst_ref=rcv3.at[y, kind],
            send_sem=s3.at[d], recv_sem=v3.at[y, kind],
            device_id=at(zg * PAIR + c // NY, c % NY), device_id_type=MESH,
        )

    far_first = (2, 6, 1, 3, 5, 7, 4)
    for d in far_first:
        s = slot_of((here + d) % cpg, kind)
        snd3[d] = mm(pre_[s, 0], ssp) + pre_[s, 1]
        send3(d).start()
    s = slot_of(here, kind)
    rcv3[y, kind] = mm(pre_[s, 0], ssp) + pre_[s, 1]

    for d in range(1, cpg):
        c = (here + d) % cpg
        pltpu.make_async_remote_copy(
            src_ref=snd3.at[0], dst_ref=rcv3.at[c % NY, c // NY],
            send_sem=s3.at[0], recv_sem=v3.at[c % NY, c // NY],
            device_id=at(z, y), device_id_type=MESH,
        ).wait_recv()

    slots = [(h - y + NY) % NY for h in range(heads)]
    states = [(split(rcv3[h, 0]), split(rcv3[h, 1])) for h in range(heads)]
    for h, d in enumerate(slots):
        ssp, csp = states[h]
        usp = split(ub[d] - mm((wm[d, 0], wm[d, 1]), ssp))
        rsp = split(xr[d] + mm((yr[d, 0], yr[d, 1]), csp))
        for t in range(2):
            us[h, t], rs[h, t] = usp[t], rsp[t]

    part = rows // nx
    ends = [whole_decay[:, h : h + 1] * jnp.sum(rcv3[h, 0] * rcv3[h, 1], axis=0, keepdims=True) for h in range(heads)]

    def gradients(starts):
        at_rows = [pl.ds(pl.multiple_of(n * part, part), part) for n in starts]

        def take(ref, *lead, cols=slice(None)):
            got = [ref[(*lead, r, cols)] for r in at_rows]
            return got[0] if len(got) == 1 else jnp.concatenate(got, axis=0)

        def put(ref, value, *lead, cols=slice(None)):
            for n, r in enumerate(at_rows):
                ref[(*lead, r, cols)] = value[n * part : (n + 1) * part]

        bc, gc, ec = take(bcol), take(gcol), take(ecol)
        for g in range(kheads):
            ku, qu = take(kn, g), take(qn, g)
            ksp, qsp = (ks[g, 0], ks[g, 1]), (qs[g, 0], qs[g, 1])
            qhat = qu * scale
            dq_sum = dk_sum = None
            for h in range(g * rep, (g + 1) * rep):
                d = slots[h]
                (ssp, csp) = states[h]
                cols = slice(h * HD, (h + 1) * HD)
                beta, gam_h, gend_h = bc[:, h : h + 1], gc[:, h : h + 1], ec[:, h : h + 1]
                do = take(do_ref, cols=cols)
                ur, rr = (take(us, h, 0), take(us, h, 1)), (take(rs, h, 0), take(rs, h, 1))
                usp, rsp = (us[h, 0], us[h, 1]), (rs[h, 0], rs[h, 1])
                dm = mm(do, usp, NT) * take(gam, d)
                dl = mm(rr, usp, NT) * take(low_, d)
                dmt = mm(ur, head(do_ref, h), NT) * take(gamt, d)
                dlt = mm(ur, rsp, NT) * take(lowt, d)
                bk = split(bcol[:, h : h + 1] * kn[g])
                dq = mm(dm, ksp) + gam_h * mm(do, ssp, NT)
                e = mm(dl, ksp) - gam_h * mm(rr, ssp, NT)
                ug = gend_h * mm(ur, csp, NT)
                dkw = mm(dmt, qsp) + mm(dlt, bk) + ug
                left = beta * e
                dr = rr[0].astype(f32) + rr[1].astype(f32)
                put(gbuf, (beta * dr).astype(bf16), cols=slice((2 * kheads + h) * HD, (2 * kheads + h + 1) * HD))
                put(ebeta, dr * take(v_ref, cols=cols).astype(f32) + ku * e, h)
                put(ecum, qhat * dq + ku * (left - dkw), h)
                ends[h] = ends[h] + jnp.sum(ku * ug, axis=0, keepdims=True)
                dk = left + dkw
                dq_sum = dq if dq_sum is None else dq_sum + dq
                dk_sum = dk if dk_sum is None else dk_sum + dk
            for x_ref, unit_rows, grad, at_col, mult in (
                (q_ref, qu, dq_sum, g, scale), (k_ref, ku, dk_sum, kheads + g, 1.0),
            ):
                xf = take(x_ref, cols=slice(g * HD, (g + 1) * HD)).astype(f32)
                r = lax.rsqrt(jnp.sum(xf * xf, axis=1, keepdims=True) + 1e-6) * mult
                out = r * (grad - unit_rows * jnp.sum(unit_rows * grad, axis=1, keepdims=True))
                put(gbuf, out.astype(bf16), cols=slice(at_col * HD, (at_col + 1) * HD))

    far = (me + 2) % nx
    gradients([far])
    for load in loads:
        load.wait()
    half = wq.shape[0] // 2
    kw = kheads * HD

    def project(dest, side):
        grads = gbuf[pl.ds(pl.multiple_of(dest * part, part), part), :]
        outs = slice(side * half, (side + 1) * half)
        total = lax.dot_general(grads[:, :kw], wq[outs, :], NT, preferred_element_type=f32)
        total += lax.dot_general(grads[:, kw : 2 * kw], wk[outs, :], NT, preferred_element_type=f32)
        total += lax.dot_general(grads[:, 2 * kw :], wv[outs, :], NT, preferred_element_type=f32)
        return total

    def hop(src, dst, n, to):
        return pltpu.make_async_remote_copy(
            src_ref=src, dst_ref=dst, send_sem=s4.at[n], recv_sem=v4.at[n],
            device_id={"head": to}, device_id_type=MESH,
        )

    hops = [
        hop(pd2.at[0], r2.at[0], 0, up), hop(pd2.at[1], r2.at[1], 1, down),
        hop(pr.at[1], rin.at[0, 1], 2, up), hop(pl_.at[0], rin.at[1, 0], 3, down),
        hop(pr.at[0], rin.at[0, 0], 4, up), hop(pl_.at[1], rin.at[1, 1], 5, down),
    ]
    pd2[0] = project(far, 0)
    hops[0].start()
    pd2[1] = project(far, 1)
    hops[1].start()
    gradients([up, down])
    pr[1] = project(up, 1)
    hops[2].start()
    pl_[0] = project(down, 0)
    hops[3].start()
    pr[0] = project(up, 0)
    pl_[1] = project(down, 1)
    hops[0].wait_recv()
    pr[0] = pr[0] + r2[0]
    hops[4].start()
    hops[1].wait_recv()
    pl_[1] = pl_[1] + r2[1]
    hops[5].start()
    gradients([me])
    own = [project(me, 0), project(me, 1)]
    ones = jnp.ones((16, HD), bf16)
    for h in range(heads):
        rate = mm(ones, ebeta[h], NT, 3)
        dbe_ref[h : h + 1, :] = rate[:1, :]
        dld = mm(mm(ones, ecum[h], NT, 3), tri, NN, 3) + jnp.sum(ends[h], axis=1, keepdims=True)
        dld_ref[h : h + 1, :] = dld[:1, :]
    for n in (2, 3, 4, 5):
        hops[n].wait_recv()
    for side in range(2):
        total = own[side] + rin[0, side] + rin[1, side]
        ig_ref[:, side * half : (side + 1) * half] = total.astype(bf16)

    for n in range(6):
        hops[n].wait_send()
    for d in range(1, cpg):
        send3(d).wait_send()
    for src in range(groups - 1):
        @pl.when(pos == src)
        def _():
            for dst in range(src + 1, groups):
                send2(src, dst).wait_send()
    for copy in sends1:
        copy.wait_send()


def hand_on(ig_ref, dld_ref, dbe_ref, ig_out, dld_out, dbe_out):
    ig_out[...] = ig_ref[...]
    dld_out[...] = dld_ref[...]
    dbe_out[...] = dbe_ref[...]


def solution(mesh):
    nx = mesh.shape["head"]
    groups = mesh.shape["ctx"] // (NY * PAIR)

    def per_device(q, k, v, do, ld, be, wq, wk, wv):
        rows, heads = q.shape[0], ld.shape[0]
        kheads = q.shape[1] // HD
        model = wq.shape[0]
        part, half = rows // nx, model // 2
        cpg = PAIR * NY
        vmem = pl.BlockSpec(memory_space=pltpu.VMEM)
        hbm = pl.BlockSpec(memory_space=pl.ANY)

        def buf(*shape, dtype=f32):
            return pltpu.VMEM(shape, dtype)

        dma = pltpu.SemaphoreType.DMA
        scratch = [
            buf(*wq.shape, dtype=bf16), buf(*wk.shape, dtype=bf16), buf(*wv.shape, dtype=bf16),
            buf(kheads, 2, rows, HD, dtype=bf16), buf(kheads, 2, rows, HD, dtype=bf16),
            buf(kheads, rows, HD), buf(kheads, rows, HD),
            buf(kheads, rows, rows), buf(kheads, rows, rows),
            buf(heads, rows, rows), buf(heads, rows, rows), buf(heads, rows, rows), buf(heads, rows, rows),
            buf(heads, rows, HD), buf(heads, 2, rows, HD, dtype=bf16), buf(heads, 2, rows, HD, dtype=bf16),
            buf(heads, rows, HD), buf(heads, 2, rows, HD, dtype=bf16),
            buf(heads, 2, rows, HD, dtype=bf16), buf(heads, 2, rows, HD, dtype=bf16),
            buf(rows, 16), buf(rows, 16), buf(rows, 16), buf(heads, rows, HD), buf(heads, rows, HD),
            buf(heads, PAIR, 2, HD, HD), buf(cpg, 2, HD, HD),
            buf(2, HD, HD), buf(groups - 1, 2, HD, HD), buf(HD, HD), buf(cpg, 2, HD, HD),
            buf(cpg, HD, HD), buf(heads, PAIR, HD, HD),
            buf(rows, (2 * kheads + heads) * HD, dtype=bf16),
            buf(2, part, half), buf(2, part, half), buf(2, part, half),
            buf(2, part, half), buf(2, 2, part, half),
            dma((3,)), dma((heads, PAIR)), dma((cpg,)), dma((groups,)), dma((groups,)),
            dma((cpg,)), dma((heads, PAIR)), dma((6,)), dma((6,)),
        ]
        outs = (
                jax.ShapeDtypeStruct((part, model), bf16),
                jax.ShapeDtypeStruct(ld.shape, f32),
                jax.ShapeDtypeStruct(be.shape, f32),
        )
        got = pl.pallas_call(
            functools.partial(kernel, nx, groups),
            out_shape=outs,
            in_specs=[vmem] * 6 + [hbm] * 3,
            out_specs=(vmem, vmem, vmem),
            scratch_shapes=scratch,
            compiler_params=pltpu.CompilerParams(
                collective_id=0, has_side_effects=True, vmem_limit_bytes=56 << 20
            ),
            name="delta_backward",
        )(q, k, v, do, ld, be, wq, wk, wv)
        return pl.pallas_call(
            hand_on, out_shape=outs, in_specs=[vmem] * 3, out_specs=(vmem, vmem, vmem), name="hand_on"
        )(*got)

    row = P(("dp", "ctx"), "head")
    gate = P("head", ("dp", "ctx"))
    weight = P(None, "head")
    return jax.shard_map(
        per_device, mesh=mesh,
        in_specs=(row, row, row, row, gate, gate, weight, weight, weight),
        out_specs=(P(("dp", "ctx", "head"), None), gate, gate),
        check_vma=False,
    )
```

```python
import functools

import jax
import jax.numpy as jnp
from jax import lax
from jax.experimental import pallas as pl
from jax.experimental.pallas import tpu as pltpu
from jax.sharding import PartitionSpec as P

MESH = pl.DeviceIdType.MESH
f32 = jnp.float32
bf16 = jnp.bfloat16
HD = 128
NY = 4
PAIR = 2
NN = (((1,), (0,)), ((), ()))
NT = (((1,), (1,)), ((), ()))
TN = (((0,), (0,)), ((), ()))


def split(x, n=2):
    if isinstance(x, (list, tuple)):
        return x
    if x.dtype == bf16:
        return [x]
    out = []
    for _ in range(n - 1):
        h = x.astype(bf16)
        out.append(h)
        x = x - h.astype(f32)
    out.append(x.astype(bf16))
    return out


def mm(a, b, dims=NN, n=2):
    a, b = split(a, n), split(b, n)
    total = None
    for i in reversed(range(len(a))):
        for j in reversed(range(len(b))):
            if i + j < n:
                term = lax.dot_general(a[i], b[j], dims, preferred_element_type=f32)
                total = term if total is None else total + term
    return total


def stacked(lefts, b):
    lefts = [split(a) for a in lefts]
    m = lefts[0][0].shape[0]
    high = lax.dot_general(
        jnp.concatenate([t for a in lefts for t in a], axis=0), b[0], NN, preferred_element_type=f32
    )
    low = None
    if len(b) > 1:
        low = lax.dot_general(
            jnp.concatenate([a[0] for a in lefts], axis=0), b[1], NN, preferred_element_type=f32
        )
    out, row = [], 0
    for n, a in enumerate(lefts):
        total = high[row : row + m]
        if low is not None:
            total = total + low[n * m : (n + 1) * m]
        if len(a) > 1:
            total = total + high[row + m : row + 2 * m]
        row += m * len(a)
        out.append(total)
    return out


def iotas(n):
    i = lax.broadcasted_iota(jnp.int32, (n, n), 0)
    j = lax.broadcasted_iota(jnp.int32, (n, n), 1)
    return i, j


def lower_inverses(blocks):
    n = HD
    i, j = iotas(n)
    eye = jnp.where(i == j, 1.0, 0.0).astype(f32)
    apart = i ^ j
    xs = [eye - jnp.where(apart == 1, b, 0.0) for b in blocks]
    level = 1
    while (1 << level) < n:
        here = (apart >> level) == 1
        xb = [x.astype(bf16) for x in xs]
        ys = [mm(jnp.where(here, b, 0.0).astype(bf16), x) for b, x in zip(blocks, xb)]
        xs = [x - mm(h, y.astype(bf16)) for x, h, y in zip(xs, xb, ys)]
        level += 1
    sp = [split(x) for x in xs]
    rs = [eye - x - mm(b, s) for b, x, s in zip(blocks, xs, sp)]
    return [x + mm(s, r) for x, s, r in zip(xs, sp, rs)]


def kernel(
    nx, groups,
    q_ref, k_ref, v_ref, do_ref, ld_ref, be_ref, wq_hbm, wk_hbm, wv_hbm,
    ig_ref, dld_ref, dbe_ref,
    wq, wk, wv, wtr, dot_, bks,
    qs, ks, qn, kn, kkb, qkb, gam, gamt, low_, lowt, ub, wm, ke, xr, yr, us, rs, ust, rst,
    bcol, gcol, ecol, ebeta, ecum,
    snd1, rcv1, snd2, rcv2, st, pre_, snd3, rcv3,
    gbuf, pd2, pr, pl_, r2, rin, kept,
    wsem, go, s1, v1, s2, v2, s3, v3, s4, v4,
):
    rows = q_ref.shape[0]
    heads = ld_ref.shape[0]
    kheads = q_ref.shape[1] // HD
    rep = heads // kheads
    ctx = lax.axis_index("ctx")
    me = lax.axis_index("head")
    z, y = ctx // NY, ctx % NY
    zg, kind = z // PAIR, z % PAIR
    cpg = PAIR * NY
    here = kind * NY + y
    pos = zg + kind * (groups - 1 - 2 * zg)
    up, down = (me + 1) % nx, (me + nx - 1) % nx

    def at(zz, yy):
        return {"ctx": zz * NY + yy}

    barrier = pltpu.get_barrier_semaphore()
    for d in range(1, cpg):
        c = (here + d) % cpg
        pl.semaphore_signal(barrier, inc=1, device_id=at(zg * PAIR + c // NY, c % NY), device_id_type=MESH)
    for d in range(1, groups):
        g = (zg + d) % groups
        pl.semaphore_signal(barrier, inc=1, device_id=at(g * PAIR + kind, y), device_id_type=MESH)
    for n in (up, down):
        pl.semaphore_signal(barrier, inc=1, device_id={"head": n}, device_id_type=MESH)
    dp = lax.axis_index("dp")
    pl.semaphore_signal(barrier, inc=1, device_id={"dp": 1 - dp}, device_id_type=MESH)

    loads = [
        pltpu.make_async_copy(a, b, wsem.at[i])
        for i, (a, b) in enumerate(((wq_hbm, wq), (wk_hbm, wk), (wv_hbm, wv)))
    ]
    for load in loads:
        load.start()

    order = (2, 1, 3, 0)
    i, j = iotas(rows)
    lower, strict = i >= j, i > j
    tri = jnp.where(lower, 1.0, 0.0).astype(bf16)
    unit = jnp.where(i == j, 1.0, 0.0).astype(bf16)

    def own_head(d):
        return (y + d) % NY

    def turned(ref):
        turn = [ref[pl.ds(own_head(d), 1), :] for d in range(heads)]
        return split(jnp.concatenate(turn * 4, axis=0), 3)

    lds = turned(ld_ref)
    c_cols = mm(tri, lds, NT, 3)
    c_rows = mm(lds, tri, NT, 3)
    b_cols = mm(unit, turned(be_ref), NT, 3)
    c_col = [c_cols[:, d : d + 1] for d in range(heads)]
    b_col = [b_cols[:, d : d + 1] for d in range(heads)]
    gamma = [jnp.exp(c) for c in c_col]
    c_end = [c[rows - 1 :, :] for c in c_col]
    gend = [jnp.exp(e - c) for e, c in zip(c_end, c_col)]

    i1, j1 = iotas(HD)
    eye = jnp.where(i1 == j1, 1.0, 0.0).astype(f32)

    scale = HD**-0.5
    for g in range(kheads):
        cols = slice(g * HD, (g + 1) * HD)
        qf, kf = q_ref[:, cols].astype(f32), k_ref[:, cols].astype(f32)
        rq = lax.rsqrt(jnp.sum(qf * qf, axis=1, keepdims=True) + 1e-6)
        rk = lax.rsqrt(jnp.sum(kf * kf, axis=1, keepdims=True) + 1e-6)
        qu, ku = qf * rq, kf * rk
        qn[g], kn[g] = qu, ku
        qsp, ksp = split(qu * scale), split(ku)
        for t in range(2):
            qs[g, t], ks[g, t] = qsp[t], ksp[t]
        kkb[g] = mm(ksp, ksp, NT)
        qkb[g] = mm(qsp, ksp, NT)

    def head(ref, h):
        return ref[:, h * HD : (h + 1) * HD]

    def turned_head(ref, d):
        return ref[:, pl.ds(pl.multiple_of(own_head(d) * HD, HD), HD)]

    def slot_of(c, kk_):
        return c + kk_ * (cpg - 1 - 2 * c)

    def send1(d, kk_):
        slot = slot_of(here, kk_)
        return pltpu.make_async_remote_copy(
            src_ref=snd1.at[d, kk_], dst_ref=rcv1.at[slot],
            send_sem=s1.at[d, kk_], recv_sem=v1.at[slot],
            device_id=at(zg * PAIR + kk_, own_head(d)), device_id_type=MESH,
        )

    sends1 = [send1(d, kk_) for d in order[:-1] for kk_ in range(PAIR)] + [send1(0, 1 - kind)]

    zero = jnp.zeros((HD, HD), bf16)
    tsps, duos = {}, {}
    for pair in (order,):
        blocks, corners, mix = [], [], []
        for d in pair:
            g = own_head(d) // rep
            w = jnp.where(lower, jnp.exp(jnp.minimum(c_col[d] - c_rows[d : d + 1, :], 0.0)), 0.0)
            gam[d] = w
            low = jnp.where(strict, w * kkb[g], 0.0) * b_col[d]
            mix.append(split(w * qkb[g]))
            blocks += [low[:HD, :HD], low[HD:, HD:]]
            corners.append(low[HD:, :HD])
        inv = [split(x) for x in lower_inverses(blocks)]
        mids = [mm(c, inv[2 * n]) for n, c in enumerate(corners)]
        inv21 = [split(-mm(inv[2 * n + 1], m)) for n, m in enumerate(mids)]
        for n, d in enumerate(pair):
            tsp = [
                jnp.concatenate(
                    [
                        jnp.concatenate([inv[2 * n][t], zero], axis=1),
                        jnp.concatenate([inv21[n][t], inv[2 * n + 1][t]], axis=1),
                    ],
                    axis=0,
                )
                for t in range(2)
            ]
            g = own_head(d) // rep
            ku, qu = kn[g], qn[g]
            do = turned_head(do_ref, d)
            right = jnp.concatenate([b_col[d] * turned_head(v_ref, d).astype(f32), (b_col[d] * gamma[d]) * ku], axis=1)
            uw = mm(tsp, right)
            ub[d] = uw[:, :HD]
            uws = split(uw)
            kend = split(gend[d] * ku)
            wsp = [t[:, HD:] for t in uws]
            for t in range(2):
                wm[d, t], ke[d, t] = wsp[t], kend[t]
            ba = mm(kend, uws, TN)
            a = jnp.exp(c_end[d]) * eye - ba[:, HD:]
            snd1[d, 0, 0] = a
            snd1[d, 0, 1] = ba[:, :HD]
            snd1[d, 1, 0] = a.T
            duo = mm(mix[n], do, TN)
            snd1[d, 1, 1] = mm((gamma[d] * scale) * qu, do, TN) - mm(wsp, duo, TN)
            tsps[d], duos[d] = tsp, duo
            if n == 0:
                pl.semaphore_wait(barrier, cpg + groups + 1)

            @pl.when(dp == 1)
            def _():
                for copy in sends1[PAIR * n : PAIR * (n + 1)]:
                    copy.start()

    rcv1[slot_of(here, kind)] = snd1[0, kind]

    for d in range(heads):
        xr[d] = mm(tsps[d], duos[d], TN)
        ysp = split(mm(tsps[d], (ke[d, 0], ke[d, 1]), TN))
        for t in range(2):
            yr[d, t] = ysp[t]
        w = gam[d]
        wt = jnp.where(i <= j, jnp.exp(jnp.minimum(c_rows[d : d + 1, :] - c_col[d], 0.0)), 0.0)
        gamt[d] = wt
        low_[d] = jnp.where(strict, -w, 0.0)
        lowt[d] = jnp.where(i < j, -wt, 0.0)
    c_cols = mm(tri, split(jnp.concatenate([ld_ref[...]] * 4, axis=0), 3), NT, 3)
    b_cols = mm(unit, split(jnp.concatenate([be_ref[...]] * 4, axis=0), 3), NT, 3)
    bcol[...] = b_cols
    gcol[...] = jnp.exp(c_cols)
    ecol[...] = jnp.exp(c_cols[rows - 1 :, :] - c_cols)
    whole_decay = jnp.exp(c_cols[rows - 1 :, :])
    for h in range(heads):
        dot_[h] = head(do_ref, h).T
        bsp = split(b_cols[:, h : h + 1] * kn[h // rep])
        for t in range(2):
            bks[h, t] = bsp[t]
    for load in loads:
        load.wait()
    wtr[: kheads * HD] = wq[...].T
    wtr[kheads * HD : 2 * kheads * HD] = wk[...].T
    wtr[2 * kheads * HD :] = wv[...].T

    @pl.when(dp == 1)
    def _():
        for copy in sends1:
            copy.wait_send()
        pl.semaphore_signal(go, inc=1, device_id={"dp": 0}, device_id_type=MESH)

    @pl.when(dp == 0)
    def _():
        pl.semaphore_wait(go, 1)
        for copy in sends1:
            copy.start()

    for d in range(1, cpg):
        s = slot_of((here + d) % cpg, kind)
        pltpu.make_async_remote_copy(
            src_ref=snd1.at[0, 0], dst_ref=rcv1.at[s], send_sem=s1.at[0, 0], recv_sem=v1.at[s],
            device_id=at(z, y), device_id_type=MESH,
        ).wait_recv()

    def after(second, first):
        (a2, b2), (a1, b1) = second, first
        r = mm(a2, jnp.concatenate([a1, b1], axis=1))
        return r[:, :HD], r[:, HD:] + b2

    maps = [(rcv1[s, 0], rcv1[s, 1]) for s in range(cpg)]
    two = [after(maps[2 * t + 1], maps[2 * t]) for t in range(cpg // 2)]
    four = [after(two[1], two[0]), after(two[3], two[2])]
    whole = after(four[1], four[0])
    snd2[0], snd2[1] = whole

    def send2(src, dst):
        gg = dst + kind * (groups - 1 - 2 * dst)
        lo = 1 if src == 0 else 0
        return pltpu.make_async_remote_copy(
            src_ref=snd2.at[lo:], dst_ref=rcv2.at[src, lo:],
            send_sem=s2.at[dst], recv_sem=v2.at[src],
            device_id=at(gg * PAIR + kind, y), device_id_type=MESH,
        )

    for src in range(groups - 1):
        @pl.when(pos == src)
        def _():
            for dst in reversed(range(src + 1, groups)):
                send2(src, dst).start()

    pre = [maps[0], two[0], after(maps[2], two[0]), four[0]]
    pre += [after(maps[4], four[0]), after(two[2], four[0])]
    pre.append(after(maps[6], pre[5]))

    pre_[0, 0] = eye
    pre_[0, 1] = jnp.zeros((HD, HD), f32)
    for n, (a, b) in enumerate(pre):
        pre_[n + 1, 0], pre_[n + 1, 1] = a, b

    st[...] = jnp.zeros_like(st)
    for dst in range(1, groups):
        @pl.when(pos == dst)
        def _():
            for src in range(dst):
                send2(src, dst).wait_recv()
            state = rcv2[0, 1]
            for src in range(1, dst):
                state = mm(rcv2[src, 0], state) + rcv2[src, 1]
            st[...] = state

    ssp = split(st[...])

    def send3(d):
        c = (here + d) % cpg
        return pltpu.make_async_remote_copy(
            src_ref=snd3.at[d], dst_ref=rcv3.at[y, kind],
            send_sem=s3.at[d], recv_sem=v3.at[y, kind],
            device_id=at(zg * PAIR + c // NY, c % NY), device_id_type=MESH,
        )

    far_first = (2, 6, 1, 3, 5, 7, 4)
    for d in far_first:
        s = slot_of((here + d) % cpg, kind)
        snd3[d] = mm(pre_[s, 0], ssp) + pre_[s, 1]
        send3(d).start()
    s = slot_of(here, kind)
    rcv3[y, kind] = mm(pre_[s, 0], ssp) + pre_[s, 1]

    for d in range(1, cpg):
        c = (here + d) % cpg
        pltpu.make_async_remote_copy(
            src_ref=snd3.at[0], dst_ref=rcv3.at[c % NY, c // NY],
            send_sem=s3.at[0], recv_sem=v3.at[c % NY, c // NY],
            device_id=at(z, y), device_id_type=MESH,
        ).wait_recv()

    slots = [(h - y + NY) % NY for h in range(heads)]
    states = [(split(rcv3[h, 0]), split(rcv3[h, 1])) for h in range(heads)]
    for h, d in enumerate(slots):
        ssp, csp = states[h]
        usp = split(ub[d] - mm((wm[d, 0], wm[d, 1]), ssp))
        rsp = split(xr[d] + mm((yr[d, 0], yr[d, 1]), csp))
        for t in range(2):
            us[h, t], rs[h, t] = usp[t], rsp[t]
            ust[h, t], rst[h, t] = usp[t].T, rsp[t].T
    turned_states = [[[t.T for t in x] for x in pair] for pair in states]

    part = rows // nx
    ends = [whole_decay[:, h : h + 1] * jnp.sum(rcv3[h, 0] * rcv3[h, 1], axis=0, keepdims=True) for h in range(heads)]

    def gradients(starts):
        at_rows = [pl.ds(pl.multiple_of(n * part, part), part) for n in starts]

        def take(ref, *lead, cols=slice(None)):
            got = [ref[(*lead, r, cols)] for r in at_rows]
            return got[0] if len(got) == 1 else jnp.concatenate(got, axis=0)

        def put(ref, value, *lead, cols=slice(None)):
            for n, r in enumerate(at_rows):
                ref[(*lead, r, cols)] = value[n * part : (n + 1) * part]

        bc, gc, ec = take(bcol), take(gcol), take(ecol)
        for g in range(kheads):
            ku, qu = take(kn, g), take(qn, g)
            ksp, qsp = (ks[g, 0], ks[g, 1]), (qs[g, 0], qs[g, 1])
            qhat = qu * scale
            dq_sum = dk_sum = None
            for h in range(g * rep, (g + 1) * rep):
                d = slots[h]
                cols = slice(h * HD, (h + 1) * HD)
                beta, gam_h, gend_h = bc[:, h : h + 1], gc[:, h : h + 1], ec[:, h : h + 1]
                do = take(do_ref, cols=cols)
                ur, rr = (take(us, h, 0), take(us, h, 1)), (take(rs, h, 0), take(rs, h, 1))
                (st_, ct_) = turned_states[h]
                both = stacked([do, rr], (ust[h, 0], ust[h, 1]))
                dm, dl = both[0] * take(gam, d), both[1] * take(low_, d)
                (dmt,) = stacked([ur], (dot_[h],))
                (dlt,) = stacked([ur], (rst[h, 0], rst[h, 1]))
                dmt, dlt = dmt * take(gamt, d), dlt * take(lowt, d)
                at_do, at_dr = stacked([do, rr], st_)
                (ug,) = stacked([ur], ct_)
                dq, e = stacked([dm, dl], ksp)
                dq, e = dq + gam_h * at_do, e - gam_h * at_dr
                ug = gend_h * ug
                dkw = stacked([dmt], qsp)[0] + stacked([dlt], (bks[h, 0], bks[h, 1]))[0] + ug
                left = beta * e
                dr = rr[0].astype(f32) + rr[1].astype(f32)
                put(gbuf, (beta * dr).astype(bf16), cols=slice((2 * kheads + h) * HD, (2 * kheads + h + 1) * HD))
                put(ebeta, dr * take(v_ref, cols=cols).astype(f32) + ku * e, h)
                put(ecum, qhat * dq + ku * (left - dkw), h)
                ends[h] = ends[h] + jnp.sum(ku * ug, axis=0, keepdims=True)
                dk = left + dkw
                dq_sum = dq if dq_sum is None else dq_sum + dq
                dk_sum = dk if dk_sum is None else dk_sum + dk
            for x_ref, unit_rows, grad, at_col, mult in (
                (q_ref, qu, dq_sum, g, scale), (k_ref, ku, dk_sum, kheads + g, 1.0),
            ):
                xf = take(x_ref, cols=slice(g * HD, (g + 1) * HD)).astype(f32)
                r = lax.rsqrt(jnp.sum(xf * xf, axis=1, keepdims=True) + 1e-6) * mult
                out = r * (grad - unit_rows * jnp.sum(unit_rows * grad, axis=1, keepdims=True))
                put(gbuf, out.astype(bf16), cols=slice(at_col * HD, (at_col + 1) * HD))

    far = (me + 2) % nx
    gradients([far])
    half = wq.shape[0] // 2

    def project(dests, start, size):
        grads = [gbuf[pl.ds(pl.multiple_of(n * part, part), part), :] for n in dests]
        grads = grads[0] if len(grads) == 1 else jnp.concatenate(grads, axis=0)
        return lax.dot_general(grads, wtr[:, start : start + size], NN, preferred_element_type=f32)

    pieces = 2
    width = half // pieces

    def hop(src, dst, n, to):
        return pltpu.make_async_remote_copy(
            src_ref=src, dst_ref=dst, send_sem=s4.at[n], recv_sem=v4.at[n],
            device_id={"head": to}, device_id_type=MESH,
        )

    cut = [slice(p * width, (p + 1) * width) for p in range(pieces)]
    first = [hop(pd2.at[0, :, c], r2.at[0, :, c], p, up) for p, c in enumerate(cut)]
    first += [hop(pd2.at[1, :, c], r2.at[1, :, c], pieces + p, down) for p, c in enumerate(cut)]
    last = [hop(pr.at[0, :, c], rin.at[0, 0, :, c], 2 * pieces + p, up) for p, c in enumerate(cut)]
    last += [hop(pl_.at[1, :, c], rin.at[1, 1, :, c], 3 * pieces + p, down) for p, c in enumerate(cut)]
    alone = [
        hop(pr.at[1], rin.at[0, 1], 4 * pieces, up), hop(pl_.at[0], rin.at[1, 0], 4 * pieces + 1, down),
    ]
    for p, c in enumerate(cut):
        for side in range(2):
            pd2[side, :, c] = project([far], side * half + p * width, width)
            first[side * pieces + p].start()
    gradients([up, down])
    both = project([up, down], half, half)
    pr[1] = both[:part]
    alone[0].start()
    pl_[1] = both[part:]
    both = project([up, down], 0, half)
    pl_[0] = both[part:]
    alone[1].start()
    pr[0] = both[:part]
    for p, c in enumerate(cut):
        first[p].wait_recv()
        pr[0, :, c] = pr[0, :, c] + r2[0, :, c]
        last[p].start()
        first[pieces + p].wait_recv()
        pl_[1, :, c] = pl_[1, :, c] + r2[1, :, c]
        last[pieces + p].start()
    gradients([me])
    own = [project([me], 0, half), project([me], half, half)]
    ones = jnp.ones((16, HD), bf16)
    for h in range(heads):
        rate = mm(ones, ebeta[h], NT, 3)
        dbe_ref[h : h + 1, :] = rate[:1, :]
        dld = mm(mm(ones, ecum[h], NT, 3), tri, NN, 3) + jnp.sum(ends[h], axis=1, keepdims=True)
        dld_ref[h : h + 1, :] = dld[:1, :]
    for copy in alone:
        copy.wait_recv()
    kept[0] = own[0] + rin[1, 0]
    kept[1] = own[1] + rin[0, 1]
    for p, c in enumerate(cut):
        last[p].wait_recv()
        ig_ref[:, c] = (rin[0, 0, :, c] + kept[0, :, c]).astype(bf16)
        last[pieces + p].wait_recv()
        ig_ref[:, half + p * width : half + (p + 1) * width] = (rin[1, 1, :, c] + kept[1, :, c]).astype(bf16)

    for copy in first + last + alone:
        copy.wait_send()
    for d in range(1, cpg):
        send3(d).wait_send()
    for src in range(groups - 1):
        @pl.when(pos == src)
        def _():
            for dst in range(src + 1, groups):
                send2(src, dst).wait_send()
    @pl.when(dp == 0)
    def _():
        for copy in sends1:
            copy.wait_send()


def hand_on(ig_ref, dld_ref, dbe_ref, ig_out, dld_out, dbe_out):
    ig_out[...] = ig_ref[...]
    dld_out[...] = dld_ref[...]
    dbe_out[...] = dbe_ref[...]


def solution(mesh):
    nx = mesh.shape["head"]
    groups = mesh.shape["ctx"] // (NY * PAIR)

    def per_device(q, k, v, do, ld, be, wq, wk, wv):
        rows, heads = q.shape[0], ld.shape[0]
        kheads = q.shape[1] // HD
        model = wq.shape[0]
        part, half = rows // nx, model // 2
        cpg = PAIR * NY
        vmem = pl.BlockSpec(memory_space=pltpu.VMEM)
        hbm = pl.BlockSpec(memory_space=pl.ANY)

        def buf(*shape, dtype=f32):
            return pltpu.VMEM(shape, dtype)

        dma = pltpu.SemaphoreType.DMA
        scratch = [
            buf(*wq.shape, dtype=bf16), buf(*wk.shape, dtype=bf16), buf(*wv.shape, dtype=bf16),
            buf((2 * kheads + heads) * HD, model, dtype=bf16),
            buf(heads, HD, rows, dtype=bf16), buf(heads, 2, rows, HD, dtype=bf16),
            buf(kheads, 2, rows, HD, dtype=bf16), buf(kheads, 2, rows, HD, dtype=bf16),
            buf(kheads, rows, HD), buf(kheads, rows, HD),
            buf(kheads, rows, rows), buf(kheads, rows, rows),
            buf(heads, rows, rows), buf(heads, rows, rows), buf(heads, rows, rows), buf(heads, rows, rows),
            buf(heads, rows, HD), buf(heads, 2, rows, HD, dtype=bf16), buf(heads, 2, rows, HD, dtype=bf16),
            buf(heads, rows, HD), buf(heads, 2, rows, HD, dtype=bf16),
            buf(heads, 2, rows, HD, dtype=bf16), buf(heads, 2, rows, HD, dtype=bf16),
            buf(heads, 2, HD, rows, dtype=bf16), buf(heads, 2, HD, rows, dtype=bf16),
            buf(rows, 16), buf(rows, 16), buf(rows, 16), buf(heads, rows, HD), buf(heads, rows, HD),
            buf(heads, PAIR, 2, HD, HD), buf(cpg, 2, HD, HD),
            buf(2, HD, HD), buf(groups - 1, 2, HD, HD), buf(HD, HD), buf(cpg, 2, HD, HD),
            buf(cpg, HD, HD), buf(heads, PAIR, HD, HD),
            buf(rows, (2 * kheads + heads) * HD, dtype=bf16),
            buf(2, part, half), buf(2, part, half), buf(2, part, half),
            buf(2, part, half), buf(2, 2, part, half), buf(2, part, half),
            dma((3,)), pltpu.SemaphoreType.REGULAR, dma((heads, PAIR)), dma((cpg,)), dma((groups,)), dma((groups,)),
            dma((cpg,)), dma((heads, PAIR)), dma((10,)), dma((10,)),
        ]
        outs = (
                jax.ShapeDtypeStruct((part, model), bf16),
                jax.ShapeDtypeStruct(ld.shape, f32),
                jax.ShapeDtypeStruct(be.shape, f32),
        )
        got = pl.pallas_call(
            functools.partial(kernel, nx, groups),
            out_shape=outs,
            in_specs=[vmem] * 6 + [hbm] * 3,
            out_specs=(vmem, vmem, vmem),
            scratch_shapes=scratch,
            compiler_params=pltpu.CompilerParams(
                collective_id=0, has_side_effects=True, vmem_limit_bytes=56 << 20
            ),
            name="delta_backward",
        )(q, k, v, do, ld, be, wq, wk, wv)
        return pl.pallas_call(
            hand_on, out_shape=outs, in_specs=[vmem] * 3, out_specs=(vmem, vmem, vmem), name="hand_on"
        )(*got)

    row = P(("dp", "ctx"), "head")
    gate = P("head", ("dp", "ctx"))
    weight = P(None, "head")
    return jax.shard_map(
        per_device, mesh=mesh,
        in_specs=(row, row, row, row, gate, gate, weight, weight, weight),
        out_specs=(P(("dp", "ctx", "head"), None), gate, gate),
        check_vma=False,
    )
```

```python
import functools

import jax
import jax.numpy as jnp
from jax import lax
from jax.experimental import pallas as pl
from jax.experimental.pallas import tpu as pltpu
from jax.sharding import PartitionSpec as P

MESH = pl.DeviceIdType.MESH
f32 = jnp.float32
bf16 = jnp.bfloat16
HD = 128
NY = 4
PAIR = 2
NN = (((1,), (0,)), ((), ()))
NT = (((1,), (1,)), ((), ()))
TN = (((0,), (0,)), ((), ()))


def split(x, n=2):
    if isinstance(x, (list, tuple)):
        return x
    if x.dtype == bf16:
        return [x]
    out = []
    for _ in range(n - 1):
        h = x.astype(bf16)
        out.append(h)
        x = x - h.astype(f32)
    out.append(x.astype(bf16))
    return out


def mm(a, b, dims=NN, n=2):
    a, b = split(a, n), split(b, n)
    total = None
    for i in reversed(range(len(a))):
        for j in reversed(range(len(b))):
            if i + j < n:
                term = lax.dot_general(a[i], b[j], dims, preferred_element_type=f32)
                total = term if total is None else total + term
    return total


def stacked(lefts, b):
    lefts = [split(a) for a in lefts]
    m = lefts[0][0].shape[0]
    high = lax.dot_general(
        jnp.concatenate([t for a in lefts for t in a], axis=0), b[0], NN, preferred_element_type=f32
    )
    low = None
    if len(b) > 1:
        low = lax.dot_general(
            jnp.concatenate([a[0] for a in lefts], axis=0), b[1], NN, preferred_element_type=f32
        )
    out, row = [], 0
    for n, a in enumerate(lefts):
        total = high[row : row + m]
        if low is not None:
            total = total + low[n * m : (n + 1) * m]
        if len(a) > 1:
            total = total + high[row + m : row + 2 * m]
        row += m * len(a)
        out.append(total)
    return out


def iotas(n):
    i = lax.broadcasted_iota(jnp.int32, (n, n), 0)
    j = lax.broadcasted_iota(jnp.int32, (n, n), 1)
    return i, j


def lower_inverses(blocks):
    n = HD
    i, j = iotas(n)
    eye = jnp.where(i == j, 1.0, 0.0).astype(f32)
    apart = i ^ j
    xs = [eye - jnp.where(apart == 1, b, 0.0) for b in blocks]
    level = 1
    while (1 << level) < n:
        here = (apart >> level) == 1
        xb = [x.astype(bf16) for x in xs]
        ys = [mm(jnp.where(here, b, 0.0).astype(bf16), x) for b, x in zip(blocks, xb)]
        xs = [x - mm(h, y.astype(bf16)) for x, h, y in zip(xs, xb, ys)]
        level += 1
    sp = [split(x) for x in xs]
    rs = [eye - x - mm(b, s) for b, x, s in zip(blocks, xs, sp)]
    return [x + mm(s, r) for x, s, r in zip(xs, sp, rs)]


def kernel(
    nx, groups,
    q_ref, k_ref, v_ref, do_ref, ld_ref, be_ref, wq_hbm, wk_hbm, wv_hbm,
    ig_ref, dld_ref, dbe_ref,
    wq, wk, wv, wtr, dot_, bks,
    qs, ks, qn, kn, kkb, qkb, gam, gamt, low_, lowt, ub, wm, ke, xr, yr, us, rs, ust, rst,
    bcol, gcol, ecol, ebeta, ecum,
    snd1, rcv1, snd2, rcv2, st, pre_, snd3, rcv3,
    gbuf, pd2, pr, pl_, r2, rin, kept,
    wsem, go, s1, v1, s2, v2, s3, v3, s4, v4,
):
    rows = q_ref.shape[0]
    heads = ld_ref.shape[0]
    kheads = q_ref.shape[1] // HD
    rep = heads // kheads
    ctx = lax.axis_index("ctx")
    me = lax.axis_index("head")
    z, y = ctx // NY, ctx % NY
    zg, kind = z // PAIR, z % PAIR
    cpg = PAIR * NY
    here = kind * NY + y
    pos = zg + kind * (groups - 1 - 2 * zg)
    up, down = (me + 1) % nx, (me + nx - 1) % nx

    def at(zz, yy):
        return {"ctx": zz * NY + yy}

    barrier = pltpu.get_barrier_semaphore()
    for d in range(1, cpg):
        c = (here + d) % cpg
        pl.semaphore_signal(barrier, inc=1, device_id=at(zg * PAIR + c // NY, c % NY), device_id_type=MESH)
    for d in range(1, groups):
        g = (zg + d) % groups
        pl.semaphore_signal(barrier, inc=1, device_id=at(g * PAIR + kind, y), device_id_type=MESH)
    for n in (up, down):
        pl.semaphore_signal(barrier, inc=1, device_id={"head": n}, device_id_type=MESH)
    dp = lax.axis_index("dp")
    pl.semaphore_signal(barrier, inc=1, device_id={"dp": 1 - dp}, device_id_type=MESH)

    loads = [
        pltpu.make_async_copy(a, b, wsem.at[i])
        for i, (a, b) in enumerate(((wq_hbm, wq), (wk_hbm, wk), (wv_hbm, wv)))
    ]
    for load in loads:
        load.start()

    order = (2, 1, 3, 0)
    i, j = iotas(rows)
    lower, strict = i >= j, i > j
    tri = jnp.where(lower, 1.0, 0.0).astype(bf16)
    unit = jnp.where(i == j, 1.0, 0.0).astype(bf16)

    def own_head(d):
        return (y + d) % NY

    def turned(ref):
        turn = [ref[pl.ds(own_head(d), 1), :] for d in range(heads)]
        return split(jnp.concatenate(turn * 4, axis=0), 3)

    lds = turned(ld_ref)
    c_cols = mm(tri, lds, NT, 3)
    c_rows = mm(lds, tri, NT, 3)
    b_cols = mm(unit, turned(be_ref), NT, 3)
    c_col = [c_cols[:, d : d + 1] for d in range(heads)]
    b_col = [b_cols[:, d : d + 1] for d in range(heads)]
    gamma = [jnp.exp(c) for c in c_col]
    c_end = [c[rows - 1 :, :] for c in c_col]
    gend = [jnp.exp(e - c) for e, c in zip(c_end, c_col)]

    i1, j1 = iotas(HD)
    eye = jnp.where(i1 == j1, 1.0, 0.0).astype(f32)

    scale = HD**-0.5
    for g in range(kheads):
        cols = slice(g * HD, (g + 1) * HD)
        qf, kf = q_ref[:, cols].astype(f32), k_ref[:, cols].astype(f32)
        rq = lax.rsqrt(jnp.sum(qf * qf, axis=1, keepdims=True) + 1e-6)
        rk = lax.rsqrt(jnp.sum(kf * kf, axis=1, keepdims=True) + 1e-6)
        qu, ku = qf * rq, kf * rk
        qn[g], kn[g] = qu, ku
        qsp, ksp = split(qu * scale), split(ku)
        for t in range(2):
            qs[g, t], ks[g, t] = qsp[t], ksp[t]
        kkb[g] = mm(ksp, ksp, NT)
        qkb[g] = mm(qsp, ksp, NT)

    def head(ref, h):
        return ref[:, h * HD : (h + 1) * HD]

    def turned_head(ref, d):
        return ref[:, pl.ds(pl.multiple_of(own_head(d) * HD, HD), HD)]

    def slot_of(c, kk_):
        return c + kk_ * (cpg - 1 - 2 * c)

    def send1(d, kk_):
        slot = slot_of(here, kk_)
        return pltpu.make_async_remote_copy(
            src_ref=snd1.at[d, kk_], dst_ref=rcv1.at[slot],
            send_sem=s1.at[d, kk_], recv_sem=v1.at[slot],
            device_id=at(zg * PAIR + kk_, own_head(d)), device_id_type=MESH,
        )

    sends1 = [send1(d, kk_) for d in order[:-1] for kk_ in range(PAIR)] + [send1(0, 1 - kind)]

    zero = jnp.zeros((HD, HD), bf16)
    tsps, duos = {}, {}
    for pair in (order,):
        blocks, corners, mix = [], [], []
        for d in pair:
            g = own_head(d) // rep
            w = jnp.where(lower, jnp.exp(jnp.minimum(c_col[d] - c_rows[d : d + 1, :], 0.0)), 0.0)
            gam[d] = w
            low = jnp.where(strict, w * kkb[g], 0.0) * b_col[d]
            mix.append(split(w * qkb[g]))
            blocks += [low[:HD, :HD], low[HD:, HD:]]
            corners.append(low[HD:, :HD])
        inv = [split(x) for x in lower_inverses(blocks)]
        mids = [mm(c, inv[2 * n]) for n, c in enumerate(corners)]
        inv21 = [split(-mm(inv[2 * n + 1], m)) for n, m in enumerate(mids)]
        for n, d in enumerate(pair):
            tsp = [
                jnp.concatenate(
                    [
                        jnp.concatenate([inv[2 * n][t], zero], axis=1),
                        jnp.concatenate([inv21[n][t], inv[2 * n + 1][t]], axis=1),
                    ],
                    axis=0,
                )
                for t in range(2)
            ]
            g = own_head(d) // rep
            ku, qu = kn[g], qn[g]
            do = turned_head(do_ref, d)
            right = jnp.concatenate([b_col[d] * turned_head(v_ref, d).astype(f32), (b_col[d] * gamma[d]) * ku], axis=1)
            uw = mm(tsp, right)
            ub[d] = uw[:, :HD]
            uws = split(uw)
            kend = split(gend[d] * ku)
            wsp = [t[:, HD:] for t in uws]
            for t in range(2):
                wm[d, t], ke[d, t] = wsp[t], kend[t]
            ba = mm(kend, uws, TN)
            a = jnp.exp(c_end[d]) * eye - ba[:, HD:]
            snd1[d, 0, 0] = a
            snd1[d, 0, 1] = ba[:, :HD]
            snd1[d, 1, 0] = a.T
            duo = mm(mix[n], do, TN)
            snd1[d, 1, 1] = mm((gamma[d] * scale) * qu, do, TN) - mm(wsp, duo, TN)
            tsps[d], duos[d] = tsp, duo
            if n == 0:
                pl.semaphore_wait(barrier, cpg + groups + 1)

            @pl.when(dp == 1)
            def _():
                for copy in sends1[PAIR * n : PAIR * (n + 1)]:
                    copy.start()

    rcv1[slot_of(here, kind)] = snd1[0, kind]

    for d in range(heads):
        xr[d] = mm(tsps[d], duos[d], TN)
        ysp = split(mm(tsps[d], (ke[d, 0], ke[d, 1]), TN))
        for t in range(2):
            yr[d, t] = ysp[t]
        w = gam[d]
        wt = jnp.where(i <= j, jnp.exp(jnp.minimum(c_rows[d : d + 1, :] - c_col[d], 0.0)), 0.0)
        gamt[d] = wt
        low_[d] = jnp.where(strict, -w, 0.0)
        lowt[d] = jnp.where(i < j, -wt, 0.0)
    c_cols = mm(tri, split(jnp.concatenate([ld_ref[...]] * 4, axis=0), 3), NT, 3)
    b_cols = mm(unit, split(jnp.concatenate([be_ref[...]] * 4, axis=0), 3), NT, 3)
    bcol[...] = b_cols
    gcol[...] = jnp.exp(c_cols)
    ecol[...] = jnp.exp(c_cols[rows - 1 :, :] - c_cols)
    whole_decay = jnp.exp(c_cols[rows - 1 :, :])
    for h in range(heads):
        dot_[h] = head(do_ref, h).T
        bsp = split(b_cols[:, h : h + 1] * kn[h // rep])
        for t in range(2):
            bks[h, t] = bsp[t]
    for load in loads:
        load.wait()
    wtr[: kheads * HD] = wq[...].T
    wtr[kheads * HD : 2 * kheads * HD] = wk[...].T
    wtr[2 * kheads * HD :] = wv[...].T

    @pl.when(dp == 1)
    def _():
        for copy in sends1:
            copy.wait_send()
        pl.semaphore_signal(go, inc=1, device_id={"dp": 0}, device_id_type=MESH)

    @pl.when(dp == 0)
    def _():
        pl.semaphore_wait(go, 1)
        for copy in sends1:
            copy.start()

    for d in range(1, cpg):
        s = slot_of((here + d) % cpg, kind)
        pltpu.make_async_remote_copy(
            src_ref=snd1.at[0, 0], dst_ref=rcv1.at[s], send_sem=s1.at[0, 0], recv_sem=v1.at[s],
            device_id=at(z, y), device_id_type=MESH,
        ).wait_recv()

    def after(second, first):
        (a2, b2), (a1, b1) = second, first
        r = mm(a2, jnp.concatenate([a1, b1], axis=1))
        return r[:, :HD], r[:, HD:] + b2

    maps = [(rcv1[s, 0], rcv1[s, 1]) for s in range(cpg)]
    two = [after(maps[2 * t + 1], maps[2 * t]) for t in range(cpg // 2)]
    four = [after(two[1], two[0]), after(two[3], two[2])]
    whole = after(four[1], four[0])
    snd2[0], snd2[1] = whole

    def send2(src, dst):
        gg = dst + kind * (groups - 1 - 2 * dst)
        lo = 1 if src == 0 else 0
        return pltpu.make_async_remote_copy(
            src_ref=snd2.at[lo:], dst_ref=rcv2.at[src, lo:],
            send_sem=s2.at[dst], recv_sem=v2.at[src],
            device_id=at(gg * PAIR + kind, y), device_id_type=MESH,
        )

    for src in range(groups - 1):
        @pl.when(pos == src)
        def _():
            for dst in reversed(range(src + 1, groups)):
                send2(src, dst).start()

    pre = [maps[0], two[0], after(maps[2], two[0]), four[0]]
    pre += [after(maps[4], four[0]), after(two[2], four[0])]
    pre.append(after(maps[6], pre[5]))

    pre_[0, 0] = eye
    pre_[0, 1] = jnp.zeros((HD, HD), f32)
    for n, (a, b) in enumerate(pre):
        pre_[n + 1, 0], pre_[n + 1, 1] = a, b

    st[...] = jnp.zeros_like(st)
    for dst in range(1, groups):
        @pl.when(pos == dst)
        def _():
            for src in range(dst):
                send2(src, dst).wait_recv()
            state = rcv2[0, 1]
            for src in range(1, dst):
                state = mm(rcv2[src, 0], state) + rcv2[src, 1]
            st[...] = state

    ssp = split(st[...])

    def send3(d):
        c = (here + d) % cpg
        return pltpu.make_async_remote_copy(
            src_ref=snd3.at[d], dst_ref=rcv3.at[y, kind],
            send_sem=s3.at[d], recv_sem=v3.at[y, kind],
            device_id=at(zg * PAIR + c // NY, c % NY), device_id_type=MESH,
        )

    far_first = (2, 6, 1, 3, 5, 7, 4)
    for d in far_first:
        s = slot_of((here + d) % cpg, kind)
        snd3[d] = mm(pre_[s, 0], ssp) + pre_[s, 1]
        send3(d).start()
    s = slot_of(here, kind)
    rcv3[y, kind] = mm(pre_[s, 0], ssp) + pre_[s, 1]

    for d in range(1, cpg):
        c = (here + d) % cpg
        pltpu.make_async_remote_copy(
            src_ref=snd3.at[0], dst_ref=rcv3.at[c % NY, c // NY],
            send_sem=s3.at[0], recv_sem=v3.at[c % NY, c // NY],
            device_id=at(z, y), device_id_type=MESH,
        ).wait_recv()

    slots = [(h - y + NY) % NY for h in range(heads)]
    states = [(split(rcv3[h, 0]), split(rcv3[h, 1])) for h in range(heads)]
    for h, d in enumerate(slots):
        ssp, csp = states[h]
        usp = split(ub[d] - mm((wm[d, 0], wm[d, 1]), ssp))
        rsp = split(xr[d] + mm((yr[d, 0], yr[d, 1]), csp))
        for t in range(2):
            us[h, t], rs[h, t] = usp[t], rsp[t]
            ust[h, t], rst[h, t] = usp[t].T, rsp[t].T
    turned_states = [[[t.T for t in x] for x in pair] for pair in states]

    part = rows // nx
    ends = [whole_decay[:, h : h + 1] * jnp.sum(rcv3[h, 0] * rcv3[h, 1], axis=0, keepdims=True) for h in range(heads)]

    def gradients(starts):
        at_rows = [pl.ds(pl.multiple_of(n * part, part), part) for n in starts]

        def take(ref, *lead, cols=slice(None)):
            got = [ref[(*lead, r, cols)] for r in at_rows]
            return got[0] if len(got) == 1 else jnp.concatenate(got, axis=0)

        def put(ref, value, *lead, cols=slice(None)):
            for n, r in enumerate(at_rows):
                ref[(*lead, r, cols)] = value[n * part : (n + 1) * part]

        bc, gc, ec = take(bcol), take(gcol), take(ecol)
        for g in range(kheads):
            ku, qu = take(kn, g), take(qn, g)
            ksp, qsp = (ks[g, 0], ks[g, 1]), (qs[g, 0], qs[g, 1])
            qhat = qu * scale
            dq_sum = dk_sum = None
            for h in range(g * rep, (g + 1) * rep):
                d = slots[h]
                cols = slice(h * HD, (h + 1) * HD)
                beta, gam_h, gend_h = bc[:, h : h + 1], gc[:, h : h + 1], ec[:, h : h + 1]
                do = take(do_ref, cols=cols)
                ur, rr = (take(us, h, 0), take(us, h, 1)), (take(rs, h, 0), take(rs, h, 1))
                (st_, ct_) = turned_states[h]
                both = stacked([do, rr], (ust[h, 0], ust[h, 1]))
                dm, dl = both[0] * take(gam, d), both[1] * take(low_, d)
                (dmt,) = stacked([ur], (dot_[h],))
                (dlt,) = stacked([ur], (rst[h, 0], rst[h, 1]))
                dmt, dlt = dmt * take(gamt, d), dlt * take(lowt, d)
                at_do, at_dr = stacked([do, rr], st_)
                (ug,) = stacked([ur], ct_)
                dq, e = stacked([dm, dl], ksp)
                dq, e = dq + gam_h * at_do, e - gam_h * at_dr
                ug = gend_h * ug
                dkw = stacked([dmt], qsp)[0] + stacked([dlt], (bks[h, 0], bks[h, 1]))[0] + ug
                left = beta * e
                dr = rr[0].astype(f32) + rr[1].astype(f32)
                put(gbuf, (beta * dr).astype(bf16), cols=slice((2 * kheads + h) * HD, (2 * kheads + h + 1) * HD))
                put(ebeta, dr * take(v_ref, cols=cols).astype(f32) + ku * e, h)
                put(ecum, qhat * dq + ku * (left - dkw), h)
                ends[h] = ends[h] + jnp.sum(ku * ug, axis=0, keepdims=True)
                dk = left + dkw
                dq_sum = dq if dq_sum is None else dq_sum + dq
                dk_sum = dk if dk_sum is None else dk_sum + dk
            for x_ref, unit_rows, grad, at_col, mult in (
                (q_ref, qu, dq_sum, g, scale), (k_ref, ku, dk_sum, kheads + g, 1.0),
            ):
                xf = take(x_ref, cols=slice(g * HD, (g + 1) * HD)).astype(f32)
                r = lax.rsqrt(jnp.sum(xf * xf, axis=1, keepdims=True) + 1e-6) * mult
                out = r * (grad - unit_rows * jnp.sum(unit_rows * grad, axis=1, keepdims=True))
                put(gbuf, out.astype(bf16), cols=slice(at_col * HD, (at_col + 1) * HD))

    far = (me + 2) % nx
    gradients([far])
    half = wq.shape[0] // 2

    def project(dests, start, size):
        grads = [gbuf[pl.ds(pl.multiple_of(n * part, part), part), :] for n in dests]
        grads = grads[0] if len(grads) == 1 else jnp.concatenate(grads, axis=0)
        return lax.dot_general(grads, wtr[:, start : start + size], NN, preferred_element_type=f32)

    pieces = 2
    width = half // pieces

    def hop(src, dst, n, to):
        return pltpu.make_async_remote_copy(
            src_ref=src, dst_ref=dst, send_sem=s4.at[n], recv_sem=v4.at[n],
            device_id={"head": to}, device_id_type=MESH,
        )

    cut = [slice(p * width, (p + 1) * width) for p in range(pieces)]
    first = [hop(pd2.at[0, :, c], r2.at[0, :, c], p, up) for p, c in enumerate(cut)]
    first += [hop(pd2.at[1, :, c], r2.at[1, :, c], pieces + p, down) for p, c in enumerate(cut)]
    last = [hop(pr.at[0, :, c], rin.at[0, 0, :, c], 2 * pieces + p, up) for p, c in enumerate(cut)]
    last += [hop(pl_.at[1, :, c], rin.at[1, 1, :, c], 3 * pieces + p, down) for p, c in enumerate(cut)]
    alone = [
        hop(pr.at[1], rin.at[0, 1], 4 * pieces, up), hop(pl_.at[0], rin.at[1, 0], 4 * pieces + 1, down),
    ]
    for p, c in enumerate(cut):
        for side in range(2):
            pd2[side, :, c] = project([far], side * half + p * width, width)
            first[side * pieces + p].start()
    gradients([up, down])
    both = project([up, down], half, half)
    pr[1] = both[:part]
    alone[0].start()
    pl_[1] = both[part:]
    both = project([up, down], 0, half)
    pl_[0] = both[part:]
    alone[1].start()
    pr[0] = both[:part]
    for p, c in enumerate(cut):
        first[p].wait_recv()
        pr[0, :, c] = pr[0, :, c] + r2[0, :, c]
        last[p].start()
        first[pieces + p].wait_recv()
        pl_[1, :, c] = pl_[1, :, c] + r2[1, :, c]
        last[pieces + p].start()
    gradients([me])
    own = [project([me], 0, half), project([me], half, half)]
    ones = jnp.ones((16, HD), bf16)
    for h in range(heads):
        rate = mm(ones, ebeta[h], NT, 3)
        dbe_ref[h : h + 1, :] = rate[:1, :]
        dld = mm(mm(ones, ecum[h], NT, 3), tri, NN, 3) + jnp.sum(ends[h], axis=1, keepdims=True)
        dld_ref[h : h + 1, :] = dld[:1, :]
    for copy in alone:
        copy.wait_recv()
    kept[0] = own[0] + rin[1, 0]
    kept[1] = own[1] + rin[0, 1]
    for p, c in enumerate(cut):
        last[p].wait_recv()
        ig_ref[:, c] = (rin[0, 0, :, c] + kept[0, :, c]).astype(bf16)
        last[pieces + p].wait_recv()
        ig_ref[:, half + p * width : half + (p + 1) * width] = (rin[1, 1, :, c] + kept[1, :, c]).astype(bf16)

    for copy in first + last + alone:
        copy.wait_send()
    for d in range(1, cpg):
        send3(d).wait_send()
    for src in range(groups - 1):
        @pl.when(pos == src)
        def _():
            for dst in range(src + 1, groups):
                send2(src, dst).wait_send()
    @pl.when(dp == 0)
    def _():
        for copy in sends1:
            copy.wait_send()


def solution(mesh):
    nx = mesh.shape["head"]
    groups = mesh.shape["ctx"] // (NY * PAIR)

    def per_device(q, k, v, do, ld, be, wq, wk, wv):
        rows, heads = q.shape[0], ld.shape[0]
        kheads = q.shape[1] // HD
        model = wq.shape[0]
        part, half = rows // nx, model // 2
        cpg = PAIR * NY
        vmem = pl.BlockSpec(memory_space=pltpu.VMEM)
        hbm = pl.BlockSpec(memory_space=pl.ANY)

        def buf(*shape, dtype=f32):
            return pltpu.VMEM(shape, dtype)

        dma = pltpu.SemaphoreType.DMA
        scratch = [
            buf(*wq.shape, dtype=bf16), buf(*wk.shape, dtype=bf16), buf(*wv.shape, dtype=bf16),
            buf((2 * kheads + heads) * HD, model, dtype=bf16),
            buf(heads, HD, rows, dtype=bf16), buf(heads, 2, rows, HD, dtype=bf16),
            buf(kheads, 2, rows, HD, dtype=bf16), buf(kheads, 2, rows, HD, dtype=bf16),
            buf(kheads, rows, HD), buf(kheads, rows, HD),
            buf(kheads, rows, rows), buf(kheads, rows, rows),
            buf(heads, rows, rows), buf(heads, rows, rows), buf(heads, rows, rows), buf(heads, rows, rows),
            buf(heads, rows, HD), buf(heads, 2, rows, HD, dtype=bf16), buf(heads, 2, rows, HD, dtype=bf16),
            buf(heads, rows, HD), buf(heads, 2, rows, HD, dtype=bf16),
            buf(heads, 2, rows, HD, dtype=bf16), buf(heads, 2, rows, HD, dtype=bf16),
            buf(heads, 2, HD, rows, dtype=bf16), buf(heads, 2, HD, rows, dtype=bf16),
            buf(rows, 16), buf(rows, 16), buf(rows, 16), buf(heads, rows, HD), buf(heads, rows, HD),
            buf(heads, PAIR, 2, HD, HD), buf(cpg, 2, HD, HD),
            buf(2, HD, HD), buf(groups - 1, 2, HD, HD), buf(HD, HD), buf(cpg, 2, HD, HD),
            buf(cpg, HD, HD), buf(heads, PAIR, HD, HD),
            buf(rows, (2 * kheads + heads) * HD, dtype=bf16),
            buf(2, part, half), buf(2, part, half), buf(2, part, half),
            buf(2, part, half), buf(2, 2, part, half), buf(2, part, half),
            dma((3,)), pltpu.SemaphoreType.REGULAR, dma((heads, PAIR)), dma((cpg,)), dma((groups,)), dma((groups,)),
            dma((cpg,)), dma((heads, PAIR)), dma((10,)), dma((10,)),
        ]
        outs = (
                jax.ShapeDtypeStruct((part, model), bf16),
                jax.ShapeDtypeStruct(ld.shape, f32),
                jax.ShapeDtypeStruct(be.shape, f32),
        )
        got = pl.pallas_call(
            functools.partial(kernel, nx, groups),
            out_shape=tuple(pltpu.VMEM(o.shape, o.dtype) for o in outs),
            in_specs=[vmem] * 6 + [hbm] * 3,
            out_specs=(vmem, vmem, vmem),
            scratch_shapes=scratch,
            compiler_params=pltpu.CompilerParams(
                collective_id=0, has_side_effects=True, vmem_limit_bytes=56 << 20
            ),
            name="delta_backward",
        )(q, k, v, do, ld, be, wq, wk, wv)
        return got

    row = P(("dp", "ctx"), "head")
    gate = P("head", ("dp", "ctx"))
    weight = P(None, "head")
    return jax.shard_map(
        per_device, mesh=mesh,
        in_specs=(row, row, row, row, gate, gate, weight, weight, weight),
        out_specs=(P(("dp", "ctx", "head"), None), gate, gate),
        check_vma=False,
    )
```

```python
import functools

import jax
import jax.numpy as jnp
from jax import lax
from jax.experimental import pallas as pl
from jax.experimental.pallas import tpu as pltpu
from jax.sharding import PartitionSpec as P

MESH = pl.DeviceIdType.MESH
f32 = jnp.float32
bf16 = jnp.bfloat16
HD = 128
NY = 4
PAIR = 2
NN = (((1,), (0,)), ((), ()))
NT = (((1,), (1,)), ((), ()))
TN = (((0,), (0,)), ((), ()))


def split(x, n=2):
    if isinstance(x, (list, tuple)):
        return x
    if x.dtype == bf16:
        return [x]
    out = []
    for _ in range(n - 1):
        h = x.astype(bf16)
        out.append(h)
        x = x - h.astype(f32)
    out.append(x.astype(bf16))
    return out


def mm(a, b, dims=NN, n=2):
    a, b = split(a, n), split(b, n)
    total = None
    for i in reversed(range(len(a))):
        for j in reversed(range(len(b))):
            if i + j < n:
                term = lax.dot_general(a[i], b[j], dims, preferred_element_type=f32)
                total = term if total is None else total + term
    return total


def stacked(lefts, b):
    lefts = [split(a) for a in lefts]
    m = lefts[0][0].shape[0]
    high = lax.dot_general(
        jnp.concatenate([t for a in lefts for t in a], axis=0), b[0], NN, preferred_element_type=f32
    )
    low = None
    if len(b) > 1:
        low = lax.dot_general(
            jnp.concatenate([a[0] for a in lefts], axis=0), b[1], NN, preferred_element_type=f32
        )
    out, row = [], 0
    for n, a in enumerate(lefts):
        total = high[row : row + m]
        if low is not None:
            total = total + low[n * m : (n + 1) * m]
        if len(a) > 1:
            total = total + high[row + m : row + 2 * m]
        row += m * len(a)
        out.append(total)
    return out


def iotas(n):
    i = lax.broadcasted_iota(jnp.int32, (n, n), 0)
    j = lax.broadcasted_iota(jnp.int32, (n, n), 1)
    return i, j


def lower_inverses(blocks):
    n = HD
    i, j = iotas(n)
    eye = jnp.where(i == j, 1.0, 0.0).astype(f32)
    apart = i ^ j
    xs = [eye - jnp.where(apart == 1, b, 0.0) for b in blocks]
    level = 1
    while (1 << level) < n:
        here = (apart >> level) == 1
        xb = [x.astype(bf16) for x in xs]
        ys = [mm(jnp.where(here, b, 0.0).astype(bf16), x) for b, x in zip(blocks, xb)]
        xs = [x - mm(h, y.astype(bf16)) for x, h, y in zip(xs, xb, ys)]
        level += 1
    sp = [split(x) for x in xs]
    rs = [eye - x - mm(b, s) for b, x, s in zip(blocks, xs, sp)]
    return [x + mm(s, r) for x, s, r in zip(xs, sp, rs)]


def kernel(
    nx, groups,
    q_ref, k_ref, v_ref, do_ref, ld_ref, be_ref, wq_hbm, wk_hbm, wv_hbm,
    ig_ref, dld_ref, dbe_ref,
    wq, wk, wv, wtr, dot_, bks,
    qs, ks, qn, kn, kkb, qkb, gam, gamt, low_, lowt, ub, wm, ke, xr, yr, us, rs, ust, rst,
    bcol, gcol, ecol, ebeta, ecum,
    snd1, rcv1, snd2, rcv2, st, pre_, snd3, rcv3,
    gbuf, pd2, pr, pl_, r2, rin, kept,
    wsem, go, s1, v1, s2, v2, s3, v3, s4, v4,
):
    rows = q_ref.shape[0]
    heads = ld_ref.shape[0]
    kheads = q_ref.shape[1] // HD
    rep = heads // kheads
    ctx = lax.axis_index("ctx")
    me = lax.axis_index("head")
    z, y = ctx // NY, ctx % NY
    zg, kind = z // PAIR, z % PAIR
    cpg = PAIR * NY
    here = kind * NY + y
    pos = zg + kind * (groups - 1 - 2 * zg)
    up, down = (me + 1) % nx, (me + nx - 1) % nx

    def at(zz, yy):
        return {"ctx": zz * NY + yy}

    barrier = pltpu.get_barrier_semaphore()
    for d in range(1, cpg):
        c = (here + d) % cpg
        pl.semaphore_signal(barrier, inc=1, device_id=at(zg * PAIR + c // NY, c % NY), device_id_type=MESH)
    for d in range(1, groups):
        g = (zg + d) % groups
        pl.semaphore_signal(barrier, inc=1, device_id=at(g * PAIR + kind, y), device_id_type=MESH)
    for n in (up, down):
        pl.semaphore_signal(barrier, inc=1, device_id={"head": n}, device_id_type=MESH)
    dp = lax.axis_index("dp")
    pl.semaphore_signal(barrier, inc=1, device_id={"dp": 1 - dp}, device_id_type=MESH)

    loads = [
        pltpu.make_async_copy(a, b, wsem.at[i])
        for i, (a, b) in enumerate(((wq_hbm, wq), (wk_hbm, wk), (wv_hbm, wv)))
    ]
    for load in loads:
        load.start()

    order = (2, 1, 3, 0)
    i, j = iotas(rows)
    lower, strict = i >= j, i > j
    tri = jnp.where(lower, 1.0, 0.0).astype(bf16)
    unit = jnp.where(i == j, 1.0, 0.0).astype(bf16)

    def own_head(d):
        return (y + d) % NY

    def turned(ref):
        turn = [ref[pl.ds(own_head(d), 1), :] for d in range(heads)]
        return split(jnp.concatenate(turn * 4, axis=0), 3)

    lds = turned(ld_ref)
    c_cols = mm(tri, lds, NT, 3)
    c_rows = mm(lds, tri, NT, 3)
    b_cols = mm(unit, turned(be_ref), NT, 3)
    c_col = [c_cols[:, d : d + 1] for d in range(heads)]
    b_col = [b_cols[:, d : d + 1] for d in range(heads)]
    gamma = [jnp.exp(c) for c in c_col]
    c_end = [c[rows - 1 :, :] for c in c_col]
    gend = [jnp.exp(e - c) for e, c in zip(c_end, c_col)]

    i1, j1 = iotas(HD)
    eye = jnp.where(i1 == j1, 1.0, 0.0).astype(f32)

    scale = HD**-0.5
    for g in range(kheads):
        cols = slice(g * HD, (g + 1) * HD)
        qf, kf = q_ref[:, cols].astype(f32), k_ref[:, cols].astype(f32)
        rq = lax.rsqrt(jnp.sum(qf * qf, axis=1, keepdims=True) + 1e-6)
        rk = lax.rsqrt(jnp.sum(kf * kf, axis=1, keepdims=True) + 1e-6)
        qu, ku = qf * rq, kf * rk
        qn[g], kn[g] = qu, ku
        qsp, ksp = split(qu * scale), split(ku)
        for t in range(2):
            qs[g, t], ks[g, t] = qsp[t], ksp[t]
        kkb[g] = mm(ksp, ksp, NT)
        qkb[g] = mm(qsp, ksp, NT)

    def head(ref, h):
        return ref[:, h * HD : (h + 1) * HD]

    def turned_head(ref, d):
        return ref[:, pl.ds(pl.multiple_of(own_head(d) * HD, HD), HD)]

    def slot_of(c, kk_):
        return c + kk_ * (cpg - 1 - 2 * c)

    def send1(d, kk_):
        slot = slot_of(here, kk_)
        return pltpu.make_async_remote_copy(
            src_ref=snd1.at[d, kk_], dst_ref=rcv1.at[slot],
            send_sem=s1.at[d, kk_], recv_sem=v1.at[slot],
            device_id=at(zg * PAIR + kk_, own_head(d)), device_id_type=MESH,
        )

    sends1 = [send1(d, kk_) for d in order[:-1] for kk_ in range(PAIR)] + [send1(0, 1 - kind)]

    zero = jnp.zeros((HD, HD), bf16)
    tsps, duos = {}, {}
    for pair in (order,):
        blocks, corners, mix = [], [], []
        for d in pair:
            g = own_head(d) // rep
            w = jnp.where(lower, jnp.exp(jnp.minimum(c_col[d] - c_rows[d : d + 1, :], 0.0)), 0.0)
            gam[d] = w
            low = jnp.where(strict, w * kkb[g], 0.0) * b_col[d]
            mix.append(split(w * qkb[g]))
            blocks += [low[:HD, :HD], low[HD:, HD:]]
            corners.append(low[HD:, :HD])
        inv = [split(x) for x in lower_inverses(blocks)]
        mids = [mm(c, inv[2 * n]) for n, c in enumerate(corners)]
        inv21 = [split(-mm(inv[2 * n + 1], m)) for n, m in enumerate(mids)]
        for n, d in enumerate(pair):
            tsp = [
                jnp.concatenate(
                    [
                        jnp.concatenate([inv[2 * n][t], zero], axis=1),
                        jnp.concatenate([inv21[n][t], inv[2 * n + 1][t]], axis=1),
                    ],
                    axis=0,
                )
                for t in range(2)
            ]
            g = own_head(d) // rep
            ku, qu = kn[g], qn[g]
            do = turned_head(do_ref, d)
            right = jnp.concatenate([b_col[d] * turned_head(v_ref, d).astype(f32), (b_col[d] * gamma[d]) * ku], axis=1)
            uw = mm(tsp, right)
            ub[d] = uw[:, :HD]
            uws = split(uw)
            kend = split(gend[d] * ku)
            wsp = [t[:, HD:] for t in uws]
            for t in range(2):
                wm[d, t], ke[d, t] = wsp[t], kend[t]
            ba = mm(kend, uws, TN)
            a = jnp.exp(c_end[d]) * eye - ba[:, HD:]
            snd1[d, 0, 0] = a
            snd1[d, 0, 1] = ba[:, :HD]
            snd1[d, 1, 0] = a.T
            duo = mm(mix[n], do, TN)
            snd1[d, 1, 1] = mm((gamma[d] * scale) * qu, do, TN) - mm(wsp, duo, TN)
            tsps[d], duos[d] = tsp, duo
            if n == 0:
                pl.semaphore_wait(barrier, cpg + groups + 1)

            @pl.when(dp == 1)
            def _():
                for copy in sends1[PAIR * n : PAIR * (n + 1)]:
                    copy.start()

    rcv1[slot_of(here, kind)] = snd1[0, kind]

    for d in range(heads):
        xr[d] = mm(tsps[d], duos[d], TN)
        ysp = split(mm(tsps[d], (ke[d, 0], ke[d, 1]), TN))
        for t in range(2):
            yr[d, t] = ysp[t]
        w = gam[d]
        wt = jnp.where(i <= j, jnp.exp(jnp.minimum(c_rows[d : d + 1, :] - c_col[d], 0.0)), 0.0)
        gamt[d] = wt
        low_[d] = jnp.where(strict, -w, 0.0)
        lowt[d] = jnp.where(i < j, -wt, 0.0)
    c_cols = mm(tri, split(jnp.concatenate([ld_ref[...]] * 4, axis=0), 3), NT, 3)
    b_cols = mm(unit, split(jnp.concatenate([be_ref[...]] * 4, axis=0), 3), NT, 3)
    bcol[...] = b_cols
    gcol[...] = jnp.exp(c_cols)
    ecol[...] = jnp.exp(c_cols[rows - 1 :, :] - c_cols)
    whole_decay = jnp.exp(c_cols[rows - 1 :, :])
    for h in range(heads):
        dot_[h] = head(do_ref, h).T
        bsp = split(b_cols[:, h : h + 1] * kn[h // rep])
        for t in range(2):
            bks[h, t] = bsp[t]
    for load in loads:
        load.wait()
    wtr[: kheads * HD] = wq[...].T
    wtr[kheads * HD : 2 * kheads * HD] = wk[...].T
    wtr[2 * kheads * HD :] = wv[...].T

    @pl.when(dp == 1)
    def _():
        for copy in sends1:
            copy.wait_send()
        pl.semaphore_signal(go, inc=1, device_id={"dp": 0}, device_id_type=MESH)

    @pl.when(dp == 0)
    def _():
        pl.semaphore_wait(go, 1)
        for copy in sends1:
            copy.start()

    for d in range(1, cpg):
        s = slot_of((here + d) % cpg, kind)
        pltpu.make_async_remote_copy(
            src_ref=snd1.at[0, 0], dst_ref=rcv1.at[s], send_sem=s1.at[0, 0], recv_sem=v1.at[s],
            device_id=at(z, y), device_id_type=MESH,
        ).wait_recv()

    def after(second, first):
        (a2, b2), (a1, b1) = second, first
        r = mm(a2, jnp.concatenate([a1, b1], axis=1))
        return r[:, :HD], r[:, HD:] + b2

    maps = [(rcv1[s, 0], rcv1[s, 1]) for s in range(cpg)]
    two = [after(maps[2 * t + 1], maps[2 * t]) for t in range(cpg // 2)]
    four = [after(two[1], two[0]), after(two[3], two[2])]
    whole = after(four[1], four[0])
    snd2[0], snd2[1] = whole

    def send2(src, dst):
        gg = dst + kind * (groups - 1 - 2 * dst)
        lo = 1 if src == 0 else 0
        return pltpu.make_async_remote_copy(
            src_ref=snd2.at[lo:], dst_ref=rcv2.at[src, lo:],
            send_sem=s2.at[dst], recv_sem=v2.at[src],
            device_id=at(gg * PAIR + kind, y), device_id_type=MESH,
        )

    for src in range(groups - 1):
        @pl.when(pos == src)
        def _():
            for dst in reversed(range(src + 1, groups)):
                send2(src, dst).start()

    pre = [maps[0], two[0], after(maps[2], two[0]), four[0]]
    pre += [after(maps[4], four[0]), after(two[2], four[0])]
    pre.append(after(maps[6], pre[5]))

    pre_[0, 0] = eye
    pre_[0, 1] = jnp.zeros((HD, HD), f32)
    for n, (a, b) in enumerate(pre):
        pre_[n + 1, 0], pre_[n + 1, 1] = a, b

    st[...] = jnp.zeros_like(st)
    for dst in range(1, groups):
        @pl.when(pos == dst)
        def _():
            for src in range(dst):
                send2(src, dst).wait_recv()
            state = rcv2[0, 1]
            for src in range(1, dst):
                state = mm(rcv2[src, 0], state) + rcv2[src, 1]
            st[...] = state

    ssp = split(st[...])

    def send3(d):
        c = (here + d) % cpg
        return pltpu.make_async_remote_copy(
            src_ref=snd3.at[d], dst_ref=rcv3.at[y, kind],
            send_sem=s3.at[d], recv_sem=v3.at[y, kind],
            device_id=at(zg * PAIR + c // NY, c % NY), device_id_type=MESH,
        )

    far_first = (2, 6, 1, 3, 5, 7, 4)
    for d in far_first:
        s = slot_of((here + d) % cpg, kind)
        snd3[d] = mm(pre_[s, 0], ssp) + pre_[s, 1]
        send3(d).start()
    s = slot_of(here, kind)
    rcv3[y, kind] = mm(pre_[s, 0], ssp) + pre_[s, 1]

    for d in range(1, cpg):
        c = (here + d) % cpg
        pltpu.make_async_remote_copy(
            src_ref=snd3.at[0], dst_ref=rcv3.at[c % NY, c // NY],
            send_sem=s3.at[0], recv_sem=v3.at[c % NY, c // NY],
            device_id=at(z, y), device_id_type=MESH,
        ).wait_recv()

    slots = [(h - y + NY) % NY for h in range(heads)]
    states = [(split(rcv3[h, 0]), split(rcv3[h, 1])) for h in range(heads)]
    for h, d in enumerate(slots):
        ssp, csp = states[h]
        usp = split(ub[d] - mm((wm[d, 0], wm[d, 1]), ssp))
        rsp = split(xr[d] + mm((yr[d, 0], yr[d, 1]), csp))
        for t in range(2):
            us[h, t], rs[h, t] = usp[t], rsp[t]
            ust[h, t], rst[h, t] = usp[t].T, rsp[t].T
    turned_states = [[[t.T for t in x] for x in pair] for pair in states]

    part = rows // nx
    ends = [whole_decay[:, h : h + 1] * jnp.sum(rcv3[h, 0] * rcv3[h, 1], axis=0, keepdims=True) for h in range(heads)]

    def gradients(starts):
        at_rows = [pl.ds(pl.multiple_of(n * part, part), part) for n in starts]

        def take(ref, *lead, cols=slice(None)):
            got = [ref[(*lead, r, cols)] for r in at_rows]
            return got[0] if len(got) == 1 else jnp.concatenate(got, axis=0)

        def put(ref, value, *lead, cols=slice(None)):
            for n, r in enumerate(at_rows):
                ref[(*lead, r, cols)] = value[n * part : (n + 1) * part]

        bc, gc, ec = take(bcol), take(gcol), take(ecol)
        for g in range(kheads):
            ku, qu = take(kn, g), take(qn, g)
            ksp, qsp = (ks[g, 0], ks[g, 1]), (qs[g, 0], qs[g, 1])
            qhat = qu * scale
            dq_sum = dk_sum = None
            for h in range(g * rep, (g + 1) * rep):
                d = slots[h]
                cols = slice(h * HD, (h + 1) * HD)
                beta, gam_h, gend_h = bc[:, h : h + 1], gc[:, h : h + 1], ec[:, h : h + 1]
                do = take(do_ref, cols=cols)
                ur, rr = (take(us, h, 0), take(us, h, 1)), (take(rs, h, 0), take(rs, h, 1))
                (st_, ct_) = turned_states[h]
                both = stacked([do, rr], (ust[h, 0], ust[h, 1]))
                dm, dl = both[0] * take(gam, d), both[1] * take(low_, d)
                (dmt,) = stacked([ur], (dot_[h],))
                (dlt,) = stacked([ur], (rst[h, 0], rst[h, 1]))
                dmt, dlt = dmt * take(gamt, d), dlt * take(lowt, d)
                at_do, at_dr = stacked([do, rr], st_)
                (ug,) = stacked([ur], ct_)
                dq, e = stacked([dm, dl], ksp)
                dq, e = dq + gam_h * at_do, e - gam_h * at_dr
                ug = gend_h * ug
                dkw = stacked([dmt], qsp)[0] + stacked([dlt], (bks[h, 0], bks[h, 1]))[0] + ug
                left = beta * e
                dr = rr[0].astype(f32) + rr[1].astype(f32)
                put(gbuf, (beta * dr).astype(bf16), cols=slice((2 * kheads + h) * HD, (2 * kheads + h + 1) * HD))
                put(ebeta, dr * take(v_ref, cols=cols).astype(f32) + ku * e, h)
                put(ecum, qhat * dq + ku * (left - dkw), h)
                ends[h] = ends[h] + jnp.sum(ku * ug, axis=0, keepdims=True)
                dk = left + dkw
                dq_sum = dq if dq_sum is None else dq_sum + dq
                dk_sum = dk if dk_sum is None else dk_sum + dk
            for x_ref, unit_rows, grad, at_col, mult in (
                (q_ref, qu, dq_sum, g, scale), (k_ref, ku, dk_sum, kheads + g, 1.0),
            ):
                xf = take(x_ref, cols=slice(g * HD, (g + 1) * HD)).astype(f32)
                r = lax.rsqrt(jnp.sum(xf * xf, axis=1, keepdims=True) + 1e-6) * mult
                out = r * (grad - unit_rows * jnp.sum(unit_rows * grad, axis=1, keepdims=True))
                put(gbuf, out.astype(bf16), cols=slice(at_col * HD, (at_col + 1) * HD))

    far = (me + 2) % nx
    gradients([far])
    half = wq.shape[0] // 2

    def project(dests, start, size):
        grads = [gbuf[pl.ds(pl.multiple_of(n * part, part), part), :] for n in dests]
        grads = grads[0] if len(grads) == 1 else jnp.concatenate(grads, axis=0)
        return lax.dot_general(grads, wtr[:, start : start + size], NN, preferred_element_type=f32)

    pieces = 4
    width = half // pieces

    def hop(src, dst, n, to):
        return pltpu.make_async_remote_copy(
            src_ref=src, dst_ref=dst, send_sem=s4.at[n], recv_sem=v4.at[n],
            device_id={"head": to}, device_id_type=MESH,
        )

    cut = [slice(p * width, (p + 1) * width) for p in range(pieces)]
    first = [hop(pd2.at[0, :, c], r2.at[0, :, c], p, up) for p, c in enumerate(cut)]
    first += [hop(pd2.at[1, :, c], r2.at[1, :, c], pieces + p, down) for p, c in enumerate(cut)]
    last = [hop(pr.at[0, :, c], rin.at[0, 0, :, c], 2 * pieces + p, up) for p, c in enumerate(cut)]
    last += [hop(pl_.at[1, :, c], rin.at[1, 1, :, c], 3 * pieces + p, down) for p, c in enumerate(cut)]
    alone = [
        hop(pr.at[1], rin.at[0, 1], 4 * pieces, up), hop(pl_.at[0], rin.at[1, 0], 4 * pieces + 1, down),
    ]
    for p, c in enumerate(cut):
        for side in range(2):
            pd2[side, :, c] = project([far], side * half + p * width, width)
            first[side * pieces + p].start()
    gradients([up, down])
    both = project([up, down], half, half)
    pr[1] = both[:part]
    alone[0].start()
    pl_[1] = both[part:]
    both = project([up, down], 0, half)
    pl_[0] = both[part:]
    alone[1].start()
    pr[0] = both[:part]
    for p, c in enumerate(cut):
        first[p].wait_recv()
        pr[0, :, c] = pr[0, :, c] + r2[0, :, c]
        last[p].start()
        first[pieces + p].wait_recv()
        pl_[1, :, c] = pl_[1, :, c] + r2[1, :, c]
        last[pieces + p].start()
    gradients([me])
    own = [project([me], 0, half), project([me], half, half)]
    ones = jnp.ones((16, HD), bf16)
    for h in range(heads):
        rate = mm(ones, ebeta[h], NT, 3)
        dbe_ref[h : h + 1, :] = rate[:1, :]
        dld = mm(mm(ones, ecum[h], NT, 3), tri, NN, 3) + jnp.sum(ends[h], axis=1, keepdims=True)
        dld_ref[h : h + 1, :] = dld[:1, :]
    for copy in alone:
        copy.wait_recv()
    kept[0] = own[0] + rin[1, 0]
    kept[1] = own[1] + rin[0, 1]
    for p, c in enumerate(cut):
        last[p].wait_recv()
        ig_ref[:, c] = (rin[0, 0, :, c] + kept[0, :, c]).astype(bf16)
        last[pieces + p].wait_recv()
        ig_ref[:, half + p * width : half + (p + 1) * width] = (rin[1, 1, :, c] + kept[1, :, c]).astype(bf16)

    for copy in first + last + alone:
        copy.wait_send()
    for d in range(1, cpg):
        send3(d).wait_send()
    for src in range(groups - 1):
        @pl.when(pos == src)
        def _():
            for dst in range(src + 1, groups):
                send2(src, dst).wait_send()
    @pl.when(dp == 0)
    def _():
        for copy in sends1:
            copy.wait_send()


def solution(mesh):
    nx = mesh.shape["head"]
    groups = mesh.shape["ctx"] // (NY * PAIR)

    def per_device(q, k, v, do, ld, be, wq, wk, wv):
        rows, heads = q.shape[0], ld.shape[0]
        kheads = q.shape[1] // HD
        model = wq.shape[0]
        part, half = rows // nx, model // 2
        cpg = PAIR * NY
        vmem = pl.BlockSpec(memory_space=pltpu.VMEM)
        hbm = pl.BlockSpec(memory_space=pl.ANY)

        def buf(*shape, dtype=f32):
            return pltpu.VMEM(shape, dtype)

        dma = pltpu.SemaphoreType.DMA
        scratch = [
            buf(*wq.shape, dtype=bf16), buf(*wk.shape, dtype=bf16), buf(*wv.shape, dtype=bf16),
            buf((2 * kheads + heads) * HD, model, dtype=bf16),
            buf(heads, HD, rows, dtype=bf16), buf(heads, 2, rows, HD, dtype=bf16),
            buf(kheads, 2, rows, HD, dtype=bf16), buf(kheads, 2, rows, HD, dtype=bf16),
            buf(kheads, rows, HD), buf(kheads, rows, HD),
            buf(kheads, rows, rows), buf(kheads, rows, rows),
            buf(heads, rows, rows), buf(heads, rows, rows), buf(heads, rows, rows), buf(heads, rows, rows),
            buf(heads, rows, HD), buf(heads, 2, rows, HD, dtype=bf16), buf(heads, 2, rows, HD, dtype=bf16),
            buf(heads, rows, HD), buf(heads, 2, rows, HD, dtype=bf16),
            buf(heads, 2, rows, HD, dtype=bf16), buf(heads, 2, rows, HD, dtype=bf16),
            buf(heads, 2, HD, rows, dtype=bf16), buf(heads, 2, HD, rows, dtype=bf16),
            buf(rows, 16), buf(rows, 16), buf(rows, 16), buf(heads, rows, HD), buf(heads, rows, HD),
            buf(heads, PAIR, 2, HD, HD), buf(cpg, 2, HD, HD),
            buf(2, HD, HD), buf(groups - 1, 2, HD, HD), buf(HD, HD), buf(cpg, 2, HD, HD),
            buf(cpg, HD, HD), buf(heads, PAIR, HD, HD),
            buf(rows, (2 * kheads + heads) * HD, dtype=bf16),
            buf(2, part, half), buf(2, part, half), buf(2, part, half),
            buf(2, part, half), buf(2, 2, part, half), buf(2, part, half),
            dma((3,)), pltpu.SemaphoreType.REGULAR, dma((heads, PAIR)), dma((cpg,)), dma((groups,)), dma((groups,)),
            dma((cpg,)), dma((heads, PAIR)), dma((18,)), dma((18,)),
        ]
        outs = (
                jax.ShapeDtypeStruct((part, model), bf16),
                jax.ShapeDtypeStruct(ld.shape, f32),
                jax.ShapeDtypeStruct(be.shape, f32),
        )
        got = pl.pallas_call(
            functools.partial(kernel, nx, groups),
            out_shape=tuple(pltpu.VMEM(o.shape, o.dtype) for o in outs),
            in_specs=[vmem] * 6 + [hbm] * 3,
            out_specs=(vmem, vmem, vmem),
            scratch_shapes=scratch,
            compiler_params=pltpu.CompilerParams(
                collective_id=0, has_side_effects=True, vmem_limit_bytes=56 << 20
            ),
            name="delta_backward",
        )(q, k, v, do, ld, be, wq, wk, wv)
        return got

    row = P(("dp", "ctx"), "head")
    gate = P("head", ("dp", "ctx"))
    weight = P(None, "head")
    return jax.shard_map(
        per_device, mesh=mesh,
        in_specs=(row, row, row, row, gate, gate, weight, weight, weight),
        out_specs=(P(("dp", "ctx", "head"), None), gate, gate),
        check_vma=False,
    )
```
